32 devices in a mesh: grp: 2 (over y), row: 4 (over z), col: 4 (over x, core).
Axes of the slice: x: 2, y: 2, z: 4, core: 2. Of those that a mesh axis runs over, the one named last changes fastest.
Arguments:
- group_rhs: float32 [2, 1024, 128], P('grp', 'row'), may hold values from -6 to 6
- group_lower: float32 [2, 1024, 1024], P('grp', 'row', 'col'), may hold values from -0.09375 to 0.09375
- group_diag_inv: float32 [2, 1024, 256], P('grp'), as said below
- group_offdiag: float32 [2, 1024, 1024], P('grp', 'row', 'col'), may hold values from -0.09375 to 0.09375
- group_rows: int32 [2, 1024], P('grp', 'row'), may hold values from 0 to 2047, as said below
- root_rhs: float32 [2048, 128], P(('grp', 'row', 'col')), may hold values from -6 to 6
- root_lower: float32 [2048, 2048], P(('grp', 'row'), 'col'), may hold values from -0.0625 to 0.0625
- root_diag_inv: float32 [2048, 512], replicated, as said below
Outputs:
- group_solution: float32 [2, 1024, 128], P('grp', 'row')
- root_solution: float32 [2048, 128], P(('grp', 'row', 'col'))
The draws below stay inside these ranges and needn't reach their ends.
Inputs may be any that keep to these rules, and one draw needn't show every extreme that they name: `group_rows`: within one group the rows are distinct and ascending. `group_diag_inv`: each stacked block is lower triangular with diagonal entries between 0.5 and 1.5. `root_diag_inv`: each stacked block is lower triangular with diagonal entries between 0.5 and 1.5.
All inputs are finite; a program needn't handle non-finite values.
Results may differ from the reference program's by a relative error of at most 0.0001.
Values sent between devices are 32-bit elements; how exact they have to be, the bound alone decides.
A program may use at most 64 MiB of HBM per device.

```python
import math
import jax
import jax.numpy as jnp
from jax import lax

NRHS = 128
W0 = 2048
W1 = 1024
P1 = 1024
G = 2
NB1 = 256
NB0 = 512
N_ROW = 4
N_COL = 4


def triangle_blocks(key, shape, block_width):
    first_key, second_key = jax.random.split(key)
    row_ids = lax.broadcasted_iota(jnp.int32, shape, len(shape) - 2) % block_width
    col_ids = lax.broadcasted_iota(jnp.int32, shape, len(shape) - 1)
    noise = jax.random.normal(first_key, shape, jnp.float32) * (0.6 / math.sqrt(block_width))
    leading = jax.random.uniform(second_key, shape, jnp.float32, 0.6, 1.5)
    return jnp.where(col_ids < row_ids, noise, jnp.where(col_ids == row_ids, leading, 0.0))


def draw_group_diag_inv(key, part):
    return triangle_blocks(key, (G, W1, NB1), NB1)


def draw_root_diag_inv(key, part):
    return triangle_blocks(key, (W0, NB0), NB0)


def pick_rows(subkey):
    return jnp.sort(jax.random.permutation(subkey, W0)[:P1])


def draw_group_rows(key, part):
    subkeys = jax.random.split(key, G)
    chosen = jax.vmap(pick_rows)(subkeys)
    return chosen.astype(jnp.int32)


def block_scale(own_key, shape, cuts, smallest, largest):
    factor_of = 1.0
    for position, blocks in cuts:
        draws = jax.random.uniform(jax.random.fold_in(jax.random.fold_in(own_key, 6), position), (blocks,), jnp.float32, smallest / len(cuts), largest / len(cuts))
        factor_of = factor_of * jnp.repeat(jnp.exp(draws), shape[position] // blocks).reshape((-1,) + (1,) * (len(shape) - 1 - position))
    return factor_of


def gaussian(own_key, shape, deviation, most, cuts=(), kind=jnp.bfloat16):
    level = block_scale(own_key, shape, cuts, -0.22, 0.18) if cuts else 1.0
    drawn = jax.random.normal(own_key, shape, jnp.float32) * deviation * level
    return jnp.minimum(jnp.maximum(drawn, -most), most).astype(kind)


def setup_inputs(seed: int = 0) -> dict:
    seeds = jax.random.split(jax.random.key(seed), 9)
    return {
        "group_rhs": gaussian(seeds[0], (G, W1, NRHS), 1.0, 6.0, ((0, 2), (1, 4)), jnp.float32),
        "group_lower": gaussian(seeds[1], (G, W1, W1), (4 * W1) ** -0.5, 0.09375, ((0, 2), (1, 4), (2, 4)), jnp.float32),
        "group_diag_inv": draw_group_diag_inv(jax.random.fold_in(seeds[8], 71), 0),
        "group_offdiag": gaussian(seeds[3], (G, P1, W1), (4 * W1) ** -0.5, 0.09375, ((0, 2), (1, 4), (2, 4)), jnp.float32),
        "group_rows": draw_group_rows(jax.random.fold_in(seeds[8], 71), 0),
        "root_rhs": gaussian(seeds[5], (W0, NRHS), 1.0, 6.0, ((0, 32),), jnp.float32),
        "root_lower": gaussian(seeds[6], (W0, W0), (4 * W0) ** -0.5, 0.0625, ((0, 8), (1, 4)), jnp.float32),
        "root_diag_inv": draw_root_diag_inv(jax.random.fold_in(seeds[8], 71), 0),
    }


def exact_dot(left, right):
    return jnp.dot(left, right, precision=lax.Precision.HIGHEST, preferred_element_type=jnp.float32)


def exact_tdot(left, right):
    return lax.dot_general(left, right, (((0,), (0,)), ((), ())), precision=lax.Precision.HIGHEST, preferred_element_type=jnp.float32)


def forward_solve(diag_inv, factor, right_side, blocks):
    span_rows = diag_inv.shape[1]
    solved = []
    for kblock in range(blocks):
        first_row = kblock * span_rows
        residue = right_side[first_row:first_row + span_rows]
        if kblock > 0:
            residue = residue - exact_dot(factor[first_row:first_row + span_rows, :first_row], jnp.concatenate(solved, axis=0))
        solved.append(exact_dot(diag_inv[first_row:first_row + span_rows], residue))
    return jnp.concatenate(solved, axis=0)


def backward_solve(diag_inv, factor, right_side, blocks):
    span_rows = diag_inv.shape[1]
    solved = [None] * blocks
    for kblock in reversed(range(blocks)):
        first_row = kblock * span_rows
        last_row = first_row + span_rows
        residue = right_side[first_row:last_row]
        if kblock < blocks - 1:
            residue = residue - exact_tdot(factor[last_row:, first_row:last_row], jnp.concatenate(solved[kblock + 1:], axis=0))
        solved[kblock] = exact_tdot(diag_inv[first_row:last_row], residue)
    return jnp.concatenate(solved, axis=0)


def reference(group_rhs, group_lower, group_diag_inv, group_offdiag, group_rows, root_rhs, root_lower, root_diag_inv):
    forward_parts = []
    update = jnp.zeros((W0, NRHS), jnp.float32)
    for member in range(G):
        solved = forward_solve(group_diag_inv[member], group_lower[member], group_rhs[member], N_ROW)
        forward_parts.append(solved)
        update = update.at[group_rows[member]].add(exact_dot(group_offdiag[member], solved))
    root_side = root_rhs - update
    root_forward = forward_solve(root_diag_inv, root_lower, root_side, N_COL)
    root_solution = backward_solve(root_diag_inv, root_lower, root_forward, N_COL)
    outputs = []
    for member in range(G):
        lifted = exact_tdot(group_offdiag[member], root_solution[group_rows[member]])
        outputs.append(backward_solve(group_diag_inv[member], group_lower[member], forward_parts[member] - lifted, N_ROW))
    return jnp.stack(outputs, axis=0), root_solution
```

```python
import functools

import jax
import jax.numpy as jnp
from jax import lax
from jax.experimental import pallas as pl
from jax.experimental.pallas import tpu as pltpu
from jax.sharding import PartitionSpec as P

CORES = 2
MESH = pl.DeviceIdType.MESH
VMEM_BYTES = 56 * 1024 * 1024


def split(a):
    high = a.astype(jnp.bfloat16)
    low = (a - high.astype(jnp.float32)).astype(jnp.bfloat16)
    return high, low


def bdot(a, b):
    return jnp.dot(a, b, preferred_element_type=jnp.float32)


def mm(a, b):
    ah, al = split(a)
    n = b.shape[1]
    w = jnp.concatenate(split(b), axis=1)
    both = bdot(ah, w) + bdot(al, w)
    return both[:, :n] + both[:, n:]


def tmm(xt, a):
    ah, al = split(a)
    n = xt.shape[0]
    v = jnp.concatenate(split(xt), axis=0)
    both = bdot(v, ah) + bdot(v, al)
    return both[:n] + both[n:]


class Sizes:
    def __init__(self, mesh_shape):
        self.G, self.R, self.C = mesh_shape["grp"], mesh_shape["row"], mesh_shape["col"]
        self.X = self.C // CORES


def here():
    return lax.axis_index("grp"), lax.axis_index("row"), lax.axis_index("col")


def remote(src, dst, ss, rs, dev):
    cp = pltpu.make_async_remote_copy(
        src_ref=src, dst_ref=dst, send_sem=ss, recv_sem=rs, device_id=dev, device_id_type=MESH
    )
    cp.start()
    return cp


def wait_on(ref, sem):
    pltpu.make_async_copy(ref, ref, sem).wait()


def greet(devs):
    barrier = pltpu.get_barrier_semaphore()
    for dev in devs:
        pl.semaphore_signal(barrier, inc=1, device_id=dev, device_id_type=MESH)
    pl.semaphore_wait(barrier, len(devs))


class Sems:
    def __init__(self, send, recv):
        self.send, self.recv, self.at = send, recv, 0

    def next(self):
        k = self.at
        self.at += 1
        return self.send.at[k], self.recv.at[k]


def plane_offsets(z):
    return [(dg, dx) for dg in range(z.G) for dx in range(z.X) if dg or dx]


def row_send(z, src, slot, sems):
    g, r, c = here()
    waits = []
    for d in range(1, z.R):
        ss, rs = sems.next()
        cp = remote(src, slot(r), ss, rs, (g, (r + d) % z.R, c))
        waits.append((cp, slot((r - d + z.R) % z.R), rs))
    return waits


def plane_send(z, slot, sems, offsets=None):
    g, r, c = here()
    x, core = c // CORES, c % CORES
    waits = []
    for dg, dx in plane_offsets(z) if offsets is None else offsets:
        ss, rs = sems.next()
        tg, tx = (g + dg) % z.G, (x + dx) % z.X
        fg, fx = (g - dg + z.G) % z.G, (x - dx + z.X) % z.X
        cp = remote(slot(g, x), slot(g, x), ss, rs, (tg, r, tx * CORES + core))
        waits.append((cp, slot(fg, fx), rs))
    return waits


def core_send(z, slot, sems):
    g, r, c = here()
    x, core = c // CORES, c % CORES
    ss, rs = sems.next()
    cp = remote(slot(core), slot(core), ss, rs, (g, r, x * CORES + 1 - core))
    return [(cp, slot(1 - core), rs)]


def arrive(waits):
    for _, ref, rs in waits:
        wait_on(ref, rs)


def sent(waits):
    for cp, _, _ in waits:
        cp.wait_send()


def pair_count(n):
    return n * (n - 1) // 2


def gather_kernel(z, spb, with_root, refs_in, refs_out, send, recv, keep):
    g, r, c = here()
    x, core = c // CORES, c % CORES
    glow, grhs, rows, rrhs = refs_in[:4]
    GL, GR, ROWS, RR = refs_out[:4]
    sems = Sems(send, recv)
    if with_root:
        devs = [
            ((g + dg) % z.G, (r + dr) % z.R, (c + dc) % z.C)
            for dg in range(z.G) for dr in range(z.R) for dc in range(z.C) if dg or dr or dc
        ]
    else:
        devs = [
            (g, (r + dr) % z.R, (c + dc) % z.C)
            for dr in range(z.R) for dc in range(z.C) if dr or dc
        ]
        devs += [
            ((g + dg) % z.G, r, (x + dx) % z.X * CORES + core)
            for dg, dx in plane_offsets(z) if dg
        ]
    greet(devs)

    locals_ = []
    for k, (src, dst) in enumerate(
        ((grhs, GR.at[r]), (rows, ROWS.at[g, r]), (rrhs, RR.at[core, g, x, r]))
    ):
        cp = pltpu.make_async_copy(src, dst, keep.at[k])
        cp.start()
        locals_.append(cp)

    def scatter(src, out_slot, holder, idx, n_pieces, groups):
        base = sems.at
        rows_each = out_slot(0, 0, 0, 0).shape[0]
        offs = [
            (dg, dr, dc)
            for dg in (range(z.G) if groups else (0,)) for dr in range(z.R) for dc in range(z.C)
        ]
        sems.at += max(n_pieces, len(offs))

        def chunk(tg, tc):
            tx, tcore = tc // CORES, tc % CORES
            q = (tcore * z.G + tg) * z.X + tx if groups else tcore * z.X + tx
            return src.at[pl.ds(pl.multiple_of(q * rows_each, 8), rows_each)]

        def copies(start):
            for k, (dg, dr, dc) in enumerate(offs):
                tg, tr, tc = (g + dg) % z.G, (r + dr) % z.R, (c + dc) % z.C
                dst = out_slot(tc % CORES, tg, tc // CORES, idx)
                if dg or dr or dc:
                    cp = pltpu.make_async_remote_copy(
                        src_ref=chunk(tg, tc), dst_ref=dst, send_sem=send.at[base + k],
                        recv_sem=recv.at[base + idx], device_id=(tg, tr, tc), device_id_type=MESH,
                    )
                    cp.start() if start else cp.wait_send()
                elif start:
                    pltpu.make_async_copy(chunk(tg, tc), dst, recv.at[base + idx]).start()

        @pl.when(holder)
        def _():
            copies(True)

        def received():
            for k in range(n_pieces):
                wait_on(out_slot(core, g, x, k), recv.at[base + k])

        def done():
            @pl.when(holder)
            def _():
                copies(False)

        return received, done

    rhs_w = row_send(z, grhs, lambda rr: GR.at[rr], sems)
    rows_w = row_send(z, rows, lambda rr: ROWS.at[g, rr], sems)
    rr_w = row_send(z, rrhs, lambda rr: RR.at[core, g, x, rr], sems)
    gl_recv, gl_done = scatter(
        glow, lambda a, b, d, k: GL.at[a, d, k], c < r, r * (r - 1) // 2 + c, pair_count(z.R), False
    )
    if with_root:
        rlow, RL = refs_in[4], refs_out[4]
        strip = g * z.R + r
        kb = strip // spb
        idx = spb * (kb * (kb - 1) // 2) + (strip - kb * spb) * kb + c
        rl_recv, rl_done = scatter(
            rlow, lambda a, b, d, k: RL.at[a, b, d, k], c < kb, idx, spb * pair_count(z.C), True
        )
    for cp in locals_:
        cp.wait()
    arrive(rows_w)
    rows_p = []
    for dg in range(1, z.G):
        ss, rs = sems.next()
        cp = remote(ROWS.at[g], ROWS.at[g], ss, rs, ((g + dg) % z.G, r, c))
        rows_p.append((cp, ROWS.at[(g - dg + z.G) % z.G], rs))
    arrive(rr_w)
    rr_p = plane_send(z, lambda gg, xx: RR.at[core, gg, xx], sems)
    gl_recv()
    gl_p = plane_send(
        z, lambda gg, xx: GL.at[core, xx], sems, [(0, dx) for dx in range(1, z.X)]
    )
    if with_root:
        rl_recv()
        rl_p = plane_send(z, lambda gg, xx: RL.at[core, gg, xx], sems)
    arrive(rr_p)
    rr_c = core_send(z, lambda a: RR.at[a], sems)
    arrive(gl_p)
    gl_c = core_send(z, lambda a: GL.at[a], sems)
    pending = [rhs_w, rows_w, rr_w, rows_p, rr_p, gl_p, rr_c, gl_c]
    late = [rhs_w, rows_p, rr_c, gl_c]
    if with_root:
        arrive(rl_p)
        rl_c = core_send(z, lambda a: RL.at[a], sems)
        pending += [rl_p, rl_c]
        late += [rl_c]
    for w in late:
        arrive(w)
    for w in pending:
        sent(w)
    gl_done()
    if with_root:
        rl_done()


def gather_all(z, spb, with_root, glow, grhs, rows, rrhs, rlow):
    f32 = jnp.float32
    b1, n = grhs.shape
    ins = [glow, grhs, rows, rrhs] + ([rlow] if with_root else [])
    outs = [
        jax.ShapeDtypeStruct((CORES, z.X, pair_count(z.R), b1 // z.C, b1), f32),
        jax.ShapeDtypeStruct((z.R, b1, n), f32),
        jax.ShapeDtypeStruct((z.G, z.R, 1, b1), jnp.int32),
        jax.ShapeDtypeStruct((CORES, z.G, z.X, z.R) + rrhs.shape, f32),
    ]
    if with_root:
        s, span = rlow.shape
        outs.append(
            jax.ShapeDtypeStruct(
                (CORES, z.G, z.X, spb * pair_count(z.C), s // (z.G * z.C), span), f32
            )
        )
    n_in, n_out = len(ins), len(outs)
    n_sem = (
        4 * z.R + 2 * z.G * z.X + z.X + z.G + 4
        + max(pair_count(z.R), z.R * z.C) + max(spb * pair_count(z.C), z.G * z.R * z.C)
        + z.G * z.X
    )
    if not with_root:
        n_sem -= max(spb * pair_count(z.C), z.G * z.R * z.C)

    def body(*refs):
        gather_kernel(z, spb, with_root, refs[:n_in], refs[n_in : n_in + n_out], *refs[n_in + n_out :])

    return pl.pallas_call(
        body,
        out_shape=outs,
        in_specs=[pl.BlockSpec(memory_space=pl.ANY)] * n_in,
        out_specs=[pl.BlockSpec(memory_space=pl.ANY)] * n_out,
        scratch_shapes=[
            pltpu.SemaphoreType.DMA((n_sem,)),
            pltpu.SemaphoreType.DMA((n_sem,)),
            pltpu.SemaphoreType.DMA((3,)),
        ],
        compiler_params=pltpu.CompilerParams(collective_id=0, has_side_effects=True),
        name="gather_factors",
    )(*ins)


def update_kernel(z, part, out, got, total, send, recv, keep):
    g, r, c = here()
    x, core = c // CORES, c % CORES
    h = total.shape[0]
    sems = Sems(send, recv)
    greet(
        [(g, r, (c + d) % z.C) for d in range(1, z.C)]
        + [(g, (r + d) % z.R, c) for d in range(1, z.R)]
        + [((g + dg) % z.G, r, (x + dx) % z.X * CORES + core) for dg, dx in plane_offsets(z) if dg]
    )

    def chunk(k):
        return part.at[pl.ds(pl.multiple_of(k * h, 8), h)]

    own = pltpu.make_async_copy(chunk(c), got.at[c], keep.at[0])
    own.start()
    first = []
    for d in range(1, z.C):
        ss, rs = sems.next()
        t = (c + d) % z.C
        first.append((remote(chunk(t), got.at[c], ss, rs, (g, r, t)), got.at[(c - d + z.C) % z.C], rs))
    own.wait()
    arrive(first)
    acc = got[0]
    for k in range(1, z.C):
        acc = acc + got[k]
    total[...] = acc
    own = pltpu.make_async_copy(total, out.at[core, g, x, r], keep.at[0])
    own.start()
    second = row_send(z, total, lambda rr: out.at[core, g, x, rr], sems)
    own.wait()
    arrive(second)
    third = plane_send(z, lambda gg, xx: out.at[core, gg, xx], sems)
    arrive(third)
    fourth = core_send(z, lambda a: out.at[a], sems)
    arrive(fourth)
    for w in (first, second, third, fourth):
        sent(w)


def exchange_update(z, part):
    b1, n = part.shape
    h = b1 // z.C
    n_sem = z.C + z.R + z.G * z.X + 1
    return pl.pallas_call(
        functools.partial(update_kernel, z),
        out_shape=jax.ShapeDtypeStruct((CORES, z.G, z.X, z.R, h, n), jnp.float32),
        in_specs=[pl.BlockSpec(memory_space=pl.ANY)],
        out_specs=pl.BlockSpec(memory_space=pl.ANY),
        scratch_shapes=[
            pltpu.VMEM((z.C, h, n), jnp.float32),
            pltpu.VMEM((h, n), jnp.float32),
            pltpu.SemaphoreType.DMA((n_sem,)),
            pltpu.SemaphoreType.DMA((n_sem,)),
            pltpu.SemaphoreType.DMA((1,)),
        ],
        compiler_params=pltpu.CompilerParams(collective_id=1, has_side_effects=True),
        name="exchange_update",
    )(part)


def lifted_kernel(z, part, out, got, total, send, recv, keep):
    g, r, c = here()
    x, core = c // CORES, c % CORES
    h = total.shape[0]
    sems = Sems(send, recv)
    greet(
        [(g, (r + d) % z.R, c) for d in range(1, z.R)]
        + [(g, r, (x + dx) % z.X * CORES + core) for dx in range(1, z.X)]
        + [(g, r, x * CORES + 1 - core)]
    )

    def chunk(k):
        return part.at[pl.ds(pl.multiple_of(k * h, 8), h)]

    own = pltpu.make_async_copy(chunk(r), got.at[r], keep.at[0])
    own.start()
    first = []
    for d in range(1, z.R):
        ss, rs = sems.next()
        t = (r + d) % z.R
        first.append((remote(chunk(t), got.at[r], ss, rs, (g, t, c)), got.at[(r - d + z.R) % z.R], rs))
    own.wait()
    arrive(first)
    acc = got[0]
    for k in range(1, z.R):
        acc = acc + got[k]
    total[...] = acc
    own = pltpu.make_async_copy(total, out.at[core, x, r], keep.at[0])
    own.start()
    second = row_send(z, total, lambda rr: out.at[core, x, rr], sems)
    own.wait()
    arrive(second)
    third = plane_send(z, lambda gg, xx: out.at[core, xx], sems, [(0, dx) for dx in range(1, z.X)])
    arrive(third)
    fourth = core_send(z, lambda a: out.at[a], sems)
    arrive(fourth)
    for w in (first, second, third, fourth):
        sent(w)


def exchange_lifted(z, part):
    n, b1 = part.shape
    h = n // z.R
    n_sem = 2 * z.R + z.X + 1
    return pl.pallas_call(
        functools.partial(lifted_kernel, z),
        out_shape=jax.ShapeDtypeStruct((CORES, z.X, z.R, h, b1), jnp.float32),
        in_specs=[pl.BlockSpec(memory_space=pl.ANY)],
        out_specs=pl.BlockSpec(memory_space=pl.ANY),
        scratch_shapes=[
            pltpu.VMEM((z.R, h, b1), jnp.float32),
            pltpu.VMEM((h, b1), jnp.float32),
            pltpu.SemaphoreType.DMA((n_sem,)),
            pltpu.SemaphoreType.DMA((n_sem,)),
            pltpu.SemaphoreType.DMA((1,)),
        ],
        compiler_params=pltpu.CompilerParams(collective_id=2, has_side_effects=True),
        name="exchange_lifted",
    )(part)


def group_block(GL, k, j):
    idx = k * (k - 1) // 2 + j
    return jnp.concatenate([GL[q, idx] for q in range(GL.shape[0])], axis=0)


def forward_kernel(z, GL, GR, inv, off, y_ref, part_ref):
    b1 = inv.shape[1]
    ys = []
    for k in range(z.R):
        res = GR[k]
        for j in range(k):
            res = res - mm(group_block(GL, k, j), ys[j])
        ys.append(mm(inv[k * b1 : (k + 1) * b1], res))
        y_ref[k * b1 : (k + 1) * b1] = ys[k]
    c = lax.axis_index("col")
    own = y_ref[pl.ds(pl.multiple_of(c * b1, 8), b1)]
    part_ref[...] = mm(off[...], own)


def root_kernel(z, spb, UPD, ROWS, RR, RL, E, own_rows, off, x_ref, lift_ref, side, xt_ref):
    W0, span = E.shape
    p, n = RR.shape[-2:]
    h = UPD.shape[-2]
    b1 = h * z.C
    for g in range(z.G):
        for r in range(z.R):
            for c in range(z.C):
                at = ((g * z.R + r) * z.C + c) * p
                side[at : at + p] = RR[c % CORES, g, c // CORES, r]
    packed = []
    for g in range(z.G):
        u = jnp.concatenate(
            [UPD[c % CORES, g, c // CORES, r] for r in range(z.R) for c in range(z.C)], axis=0
        )
        packed.append(
            (
                jnp.concatenate(split(u), axis=1),
                jnp.concatenate([ROWS[g, r] for r in range(z.R)], axis=1),
            )
        )

    def block(k, j):
        pieces = []
        for s in range(spb):
            idx = spb * (k * (k - 1) // 2) + s * k + j
            pieces += [RL[q, idx] for q in range(RL.shape[0])]
        return jnp.concatenate(pieces, axis=0)

    ys = []
    for k in range(z.C):
        res = side[k * span : (k + 1) * span]
        for w, rows in packed:
            ids = lax.broadcasted_iota(jnp.int32, (span, rows.shape[1]), 0) + k * span
            hot = jnp.where(ids == rows, 1.0, 0.0).astype(jnp.bfloat16)
            both = bdot(hot, w)
            res = res - (both[:, :n] + both[:, n:])
        for j in range(k):
            res = res - mm(block(k, j), ys[j])
        ys.append(mm(E[k * span : (k + 1) * span], res))
    xs = [None] * z.C
    for k in reversed(range(z.C)):
        res = ys[k].T
        for i in range(k + 1, z.C):
            res = res - tmm(xs[i], block(i, k))
        xs[k] = tmm(res, E[k * span : (k + 1) * span])
        side[k * span : (k + 1) * span] = xs[k].T
    g, r, c = here()
    flat = (g * z.R + r) * z.C + c
    x_ref[...] = side[pl.ds(flat * p, p)]
    picked = jnp.zeros((n, b1), jnp.float32)
    for k in range(z.C):
        ids = lax.broadcasted_iota(jnp.int32, (span, b1), 0) + k * span
        hot = jnp.where(ids == own_rows[...], 1.0, 0.0).astype(jnp.bfloat16)
        both = bdot(jnp.concatenate(split(xs[k]), axis=0), hot)
        picked = picked + both[:n] + both[n:]
    lift_ref[...] = tmm(picked, off[...])


def backward_kernel(z, GL, inv, y_ref, lift, out_ref, xs_ref):
    b1 = inv.shape[1]
    xs = [None] * z.R
    for k in reversed(range(z.R)):
        lk = jnp.concatenate([lift[k % CORES, k // CORES, r] for r in range(z.R)], axis=0)
        res = y_ref[k * b1 : (k + 1) * b1].T - lk
        for i in range(k + 1, z.R):
            res = res - tmm(xs[i], group_block(GL, i, k))
        xs[k] = tmm(res, inv[k * b1 : (k + 1) * b1])
        xs_ref[k * b1 : (k + 1) * b1] = xs[k].T
    r = lax.axis_index("row")
    out_ref[...] = xs_ref[pl.ds(pl.multiple_of(r * b1, 8), b1)]


def on_chip(body, out_shape, scratch, name, *args):
    return pl.pallas_call(
        body,
        out_shape=out_shape,
        scratch_shapes=scratch,
        compiler_params=pltpu.CompilerParams(vmem_limit_bytes=VMEM_BYTES),
        name=name,
    )(*args)


def local(z, group_rhs, group_lower, group_diag_inv, group_offdiag, group_rows, root_rhs, root_lower, root_diag_inv):
    f32 = jnp.float32
    b1, n = group_rhs.shape[1:]
    width = group_diag_inv.shape[1]
    W0, span = root_diag_inv.shape
    strip = root_lower.shape[0]
    spb = span // strip
    inv, off = group_diag_inv[0], group_offdiag[0]
    with_root = strip % (8 * z.G * z.C) == 0
    got = gather_all(z, spb, with_root, group_lower[0], group_rhs[0], group_rows, root_rhs, root_lower)
    GL, GR, ROWS, RR = got[:4]
    if with_root:
        RL = got[4].reshape((z.G * z.C,) + got[4].shape[3:])
    else:
        whole = lax.all_gather(root_lower, ("grp", "row", "col"))
        whole = whole.reshape(z.G * z.R, z.C, strip, span)
        RL = jnp.stack(
            [whole[k * spb + s, j] for k in range(z.C) for s in range(spb) for j in range(k)]
        )[None]
    GL = GL.reshape((z.C,) + GL.shape[2:])
    y, part = on_chip(
        functools.partial(forward_kernel, z),
        [jax.ShapeDtypeStruct((width, n), f32), jax.ShapeDtypeStruct((b1, n), f32)],
        [], "group_forward", GL, GR, inv, off,
    )
    UPD = exchange_update(z, part)
    root_x, lift = on_chip(
        functools.partial(root_kernel, z, spb),
        [jax.ShapeDtypeStruct(root_rhs.shape, f32), jax.ShapeDtypeStruct((n, b1), f32)],
        [pltpu.VMEM((W0, n), f32), pltpu.VMEM((n, W0), f32)],
        "root_solve", UPD, ROWS, RR, RL, root_diag_inv, group_rows, off,
    )
    lifted = exchange_lifted(z, lift)
    out = on_chip(
        functools.partial(backward_kernel, z),
        jax.ShapeDtypeStruct((b1, n), f32),
        [pltpu.VMEM((width, n), f32)],
        "group_backward", GL, inv, y, lifted,
    )
    return out[None], root_x


def solution(mesh):
    z = Sizes(mesh.shape)
    placed = (
        P("grp", "row", None),
        P("grp", "row", "col"),
        P("grp", None, None),
        P("grp", "row", "col"),
        P("grp", "row"),
        P(("grp", "row", "col"), None),
        P(("grp", "row"), "col"),
        P(),
    )
    return jax.shard_map(
        functools.partial(local, z),
        mesh=mesh,
        in_specs=placed,
        out_specs=(P("grp", "row", None), P(("grp", "row", "col"), None)),
        check_vma=False,
    )
```

```python
import functools

import jax
import jax.numpy as jnp
from jax import lax
from jax.experimental import pallas as pl
from jax.experimental.pallas import tpu as pltpu
from jax.sharding import PartitionSpec as P

CORES = 2
MESH = pl.DeviceIdType.MESH
VMEM_BYTES = 56 * 1024 * 1024


def split(a):
    high = a.astype(jnp.bfloat16)
    low = (a - high.astype(jnp.float32)).astype(jnp.bfloat16)
    return high, low


def bdot(a, b):
    return jnp.dot(a, b, preferred_element_type=jnp.float32)


def mm(a, b):
    ah, al = split(a)
    n = b.shape[1]
    w = jnp.concatenate(split(b), axis=1)
    both = bdot(ah, w) + bdot(al, w)
    return both[:, :n] + both[:, n:]


def tmm(xt, a):
    ah, al = split(a)
    n = xt.shape[0]
    v = jnp.concatenate(split(xt), axis=0)
    both = bdot(v, ah) + bdot(v, al)
    return both[:n] + both[n:]


class Sizes:
    def __init__(self, mesh_shape):
        self.G, self.R, self.C = mesh_shape["grp"], mesh_shape["row"], mesh_shape["col"]
        self.X = self.C // CORES


def here():
    return lax.axis_index("grp"), lax.axis_index("row"), lax.axis_index("col")


def remote(src, dst, ss, rs, dev):
    cp = pltpu.make_async_remote_copy(
        src_ref=src, dst_ref=dst, send_sem=ss, recv_sem=rs, device_id=dev, device_id_type=MESH
    )
    cp.start()
    return cp


def wait_on(ref, sem):
    pltpu.make_async_copy(ref, ref, sem).wait()


def greet(devs):
    barrier = pltpu.get_barrier_semaphore()
    for dev in devs:
        pl.semaphore_signal(barrier, inc=1, device_id=dev, device_id_type=MESH)
    pl.semaphore_wait(barrier, len(devs))


class Sems:
    def __init__(self, send, recv):
        self.send, self.recv, self.at = send, recv, 0

    def next(self):
        k = self.at
        self.at += 1
        return self.send.at[k], self.recv.at[k]

    def block(self, n):
        self.at += n
        return self.at - n


def plane_offsets(z):
    return [(dg, dx) for dg in range(z.G) for dx in range(z.X) if dg or dx]


def row_send(z, src, slot, sems):
    g, r, c = here()
    waits = []
    for d in range(1, z.R):
        ss, rs = sems.next()
        cp = remote(src, slot(r), ss, rs, (g, (r + d) % z.R, c))
        waits.append((cp, slot((r - d + z.R) % z.R), rs))
    return waits


def plane_send(z, slot, sems, offsets=None):
    g, r, c = here()
    x, core = c // CORES, c % CORES
    waits = []
    for dg, dx in plane_offsets(z) if offsets is None else offsets:
        ss, rs = sems.next()
        tg, tx = (g + dg) % z.G, (x + dx) % z.X
        fg, fx = (g - dg + z.G) % z.G, (x - dx + z.X) % z.X
        cp = remote(slot(g, x), slot(g, x), ss, rs, (tg, r, tx * CORES + core))
        waits.append((cp, slot(fg, fx), rs))
    return waits


def core_send(z, slot, sems):
    g, r, c = here()
    x, core = c // CORES, c % CORES
    ss, rs = sems.next()
    cp = remote(slot(core), slot(core), ss, rs, (g, r, x * CORES + 1 - core))
    return [(cp, slot(1 - core), rs)]


def arrive(waits):
    for _, ref, rs in waits:
        wait_on(ref, rs)


def sent(waits):
    for cp, _, _ in waits:
        cp.wait_send()


def pair_count(n):
    return n * (n - 1) // 2


class Pieces:
    def __init__(self, z, src, slot, held, index, count, groups, forward, sems):
        self.z, self.src, self.slot, self.held, self.index = z, src, slot, held, index
        self.count, self.groups, self.forward = count, groups, forward
        g = lax.axis_index("grp")
        self.gs = range(z.G) if groups else (g,)
        self.sources = [(gs, cs) for gs in self.gs for cs in range(z.C)]
        self.plane = [(dg, dc) for dg in (range(z.G) if groups else (0,)) for dc in range(z.C)]
        self.offs = plane_offsets(z) if forward else []
        ns, no = len(self.sources), len(self.offs)
        self.send, self.recv = sems.send, sems.recv
        self.b_recv = sems.block(count)
        self.b_first = sems.block(len(self.plane))
        self.b_row = sems.block(ns * z.R)
        self.b_on = sems.block(ns * z.R * no)
        self.b_on_recv = sems.block(no * count)

    def mine(self, k):
        g, r, c = here()
        return self.slot(c % CORES, g, c // CORES, k)

    def copies(self, start):
        z = self.z
        g, r, c = here()
        k = self.index(g, r, c)
        rows_each = self.slot(0, 0, 0, 0).shape[0]

        @pl.when(self.held(g, r, c))
        def _():
            for m, (dg, dc) in enumerate(self.plane):
                tg, tc = (g + dg) % z.G, (c + dc) % z.C
                tx, tcore = tc // CORES, tc % CORES
                q = (tcore * z.G + tg) * z.X + tx if self.groups else tcore * z.X + tx
                chunk = self.src.at[pl.ds(pl.multiple_of(q * rows_each, 8), rows_each)]
                dst, rs = self.slot(tcore, tg, tx, k), self.recv.at[self.b_recv + k]
                if dg or dc:
                    cp = pltpu.make_async_remote_copy(
                        src_ref=chunk, dst_ref=dst, send_sem=self.send.at[self.b_first + m],
                        recv_sem=rs, device_id=(tg, r, tc), device_id_type=MESH,
                    )
                    cp.start() if start else cp.wait_send()
                elif start:
                    pltpu.make_async_copy(chunk, dst, rs).start()

    def onward(self, d, start):
        z = self.z
        g, r, c = here()
        x, core = c // CORES, c % CORES
        rs = (r - d + z.R) % z.R
        for m, (gs, cs) in enumerate(self.sources):
            k = self.index(gs, rs, cs)

            @pl.when(self.held(gs, rs, cs))
            def _():
                if start:
                    wait_on(self.mine(k), self.recv.at[self.b_recv + k])
                targets = []
                if d == 0:
                    for e in range(1, z.R):
                        targets.append(
                            ((g, (r + e) % z.R, c), self.b_row + m * z.R + e, self.b_recv + k)
                        )
                for o, (dg, dx) in enumerate(self.offs):
                    targets.append(
                        (
                            ((g + dg) % z.G, r, (x + dx) % z.X * CORES + core),
                            self.b_on + (d * len(self.sources) + m) * len(self.offs) + o,
                            self.b_on_recv + o * self.count + k,
                        )
                    )
                for dev, si, ri in targets:
                    cp = pltpu.make_async_remote_copy(
                        src_ref=self.mine(k), dst_ref=self.mine(k), send_sem=self.send.at[si],
                        recv_sem=self.recv.at[ri], device_id=dev, device_id_type=MESH,
                    )
                    cp.start() if start else cp.wait_send()

    def plane_arrived(self, o):
        z = self.z
        g, r, c = here()
        x, core = c // CORES, c % CORES
        dg, dx = self.offs[o]
        fg, fx = (g - dg + z.G) % z.G, (x - dx + z.X) % z.X
        for k in range(self.count):
            wait_on(self.slot(core, fg, fx, k), self.recv.at[self.b_on_recv + o * self.count + k])
        return fg, fx

    def finish(self):
        self.copies(False)
        for d in range(self.z.R):
            self.onward(d, False)


def gather_kernel(z, spb, with_root, refs_in, refs_out, send, recv, keep):
    g, r, c = here()
    x, core = c // CORES, c % CORES
    glow, grhs, rows, rrhs = refs_in[:4]
    GL, GR, ROWS, RR = refs_out[:4]
    sems = Sems(send, recv)
    groups = range(z.G) if with_root else (0,)
    devs = [
        ((g + dg) % z.G, r, (c + dc) % z.C) for dg in groups for dc in range(z.C) if dg or dc
    ] + [(g, (r + d) % z.R, c) for d in range(1, z.R)]
    if not with_root:
        devs += [
            ((g + dg) % z.G, r, (x + dx) % z.X * CORES + core)
            for dg, dx in plane_offsets(z) if dg
        ]
    greet(devs)

    low = Pieces(
        z, glow, lambda a, b, d, k: GL.at[a, d, k], lambda gg, rr, cc: cc < rr,
        lambda gg, rr, cc: rr * (rr - 1) // 2 + cc, pair_count(z.R), False, False, sems,
    )
    low.copies(True)
    if with_root:
        rlow, RL = refs_in[4], refs_out[4]

        def index(gg, rr, cc):
            strip = gg * z.R + rr
            kb = strip // spb
            return spb * (kb * (kb - 1) // 2) + (strip - kb * spb) * kb + cc

        root = Pieces(
            z, rlow, lambda a, b, d, k: RL.at[a, b, d, k],
            lambda gg, rr, cc: cc < (gg * z.R + rr) // spb,
            index, spb * pair_count(z.C), True, True, sems,
        )
        root.copies(True)
    locals_ = []
    for k, (src, dst) in enumerate(
        ((grhs, GR.at[r]), (rows, ROWS.at[g, r]), (rrhs, RR.at[core, g, x, r]))
    ):
        cp = pltpu.make_async_copy(src, dst, keep.at[k])
        cp.start()
        locals_.append(cp)
    rhs_w = row_send(z, grhs, lambda rr: GR.at[rr], sems)
    rows_w = row_send(z, rows, lambda rr: ROWS.at[g, rr], sems)
    rr_w = row_send(z, rrhs, lambda rr: RR.at[core, g, x, rr], sems)
    low.onward(0, True)
    if with_root:
        root.onward(0, True)
    for cp in locals_:
        cp.wait()
    arrive(rows_w)
    rows_p = []
    for dg in range(1, z.G):
        ss, rs = sems.next()
        cp = remote(ROWS.at[g], ROWS.at[g], ss, rs, ((g + dg) % z.G, r, c))
        rows_p.append((cp, ROWS.at[(g - dg + z.G) % z.G], rs))
    arrive(rr_w)
    rr_p = plane_send(z, lambda gg, xx: RR.at[core, gg, xx], sems)
    for d in range(1, z.R):
        low.onward(d, True)
    gl_p = plane_send(
        z, lambda gg, xx: GL.at[core, xx], sems, [(0, dx) for dx in range(1, z.X)]
    )
    if with_root:
        for d in range(1, z.R):
            root.onward(d, True)
    arrive(rr_p)
    rr_c = core_send(z, lambda a: RR.at[a], sems)
    arrive(gl_p)
    gl_c = core_send(z, lambda a: GL.at[a], sems)
    pending = [rhs_w, rows_w, rr_w, rows_p, rr_p, gl_p, rr_c, gl_c]
    late = [rhs_w, rows_p, rr_c, gl_c]
    if with_root:
        rl_c = core_send(z, lambda a: RL.at[a, g, x], sems)
        for o in range(len(root.offs)):
            fg, fx = root.plane_arrived(o)
            rl_c += core_send(z, lambda a: RL.at[a, fg, fx], sems)
        pending += [rl_c]
        late += [rl_c]
    for w in late:
        arrive(w)
    for w in pending:
        sent(w)
    low.finish()
    if with_root:
        root.finish()


def gather_all(z, spb, with_root, glow, grhs, rows, rrhs, rlow):
    f32 = jnp.float32
    b1, n = grhs.shape
    ins = [glow, grhs, rows, rrhs] + ([rlow] if with_root else [])
    outs = [
        jax.ShapeDtypeStruct((CORES, z.X, pair_count(z.R), b1 // z.C, b1), f32),
        jax.ShapeDtypeStruct((z.R, b1, n), f32),
        jax.ShapeDtypeStruct((z.G, z.R, 1, b1), jnp.int32),
        jax.ShapeDtypeStruct((CORES, z.G, z.X, z.R) + rrhs.shape, f32),
    ]
    if with_root:
        s, span = rlow.shape
        outs.append(
            jax.ShapeDtypeStruct(
                (CORES, z.G, z.X, spb * pair_count(z.C), s // (z.G * z.C), span), f32
            )
        )
    n_in, n_out = len(ins), len(outs)
    n_sem = 4 * z.R + 2 * z.G * z.X + z.X + z.G + 4
    n_sem += pair_count(z.R) + z.C + z.C * z.R
    if with_root:
        count, ns, no = spb * pair_count(z.C), z.G * z.C, z.G * z.X - 1
        n_sem += count + ns + ns * z.R + ns * z.R * no + no * count + z.G * z.X

    def body(*refs):
        gather_kernel(z, spb, with_root, refs[:n_in], refs[n_in : n_in + n_out], *refs[n_in + n_out :])

    return pl.pallas_call(
        body,
        out_shape=outs,
        in_specs=[pl.BlockSpec(memory_space=pl.ANY)] * n_in,
        out_specs=[pl.BlockSpec(memory_space=pl.ANY)] * n_out,
        scratch_shapes=[
            pltpu.SemaphoreType.DMA((n_sem,)),
            pltpu.SemaphoreType.DMA((n_sem,)),
            pltpu.SemaphoreType.DMA((3,)),
        ],
        compiler_params=pltpu.CompilerParams(collective_id=0, has_side_effects=True),
        name="gather_factors",
    )(*ins)


def update_kernel(z, part, out, got, total, send, recv, keep):
    g, r, c = here()
    x, core = c // CORES, c % CORES
    h = total.shape[0]
    sems = Sems(send, recv)
    greet(
        [(g, r, (c + d) % z.C) for d in range(1, z.C)]
        + [(g, (r + d) % z.R, c) for d in range(1, z.R)]
        + [((g + dg) % z.G, r, (x + dx) % z.X * CORES + core) for dg, dx in plane_offsets(z) if dg]
    )

    def chunk(k):
        return part.at[pl.ds(pl.multiple_of(k * h, 8), h)]

    own = pltpu.make_async_copy(chunk(c), got.at[c], keep.at[0])
    own.start()
    first = []
    for d in range(1, z.C):
        ss, rs = sems.next()
        t = (c + d) % z.C
        first.append((remote(chunk(t), got.at[c], ss, rs, (g, r, t)), got.at[(c - d + z.C) % z.C], rs))
    own.wait()
    arrive(first)
    acc = got[0]
    for k in range(1, z.C):
        acc = acc + got[k]
    total[...] = acc
    own = pltpu.make_async_copy(total, out.at[core, g, x, r], keep.at[0])
    own.start()
    second = row_send(z, total, lambda rr: out.at[core, g, x, rr], sems)
    own.wait()
    arrive(second)
    third = plane_send(z, lambda gg, xx: out.at[core, gg, xx], sems)
    arrive(third)
    fourth = core_send(z, lambda a: out.at[a], sems)
    arrive(fourth)
    for w in (first, second, third, fourth):
        sent(w)


def exchange_update(z, part):
    b1, n = part.shape
    h = b1 // z.C
    n_sem = z.C + z.R + z.G * z.X + 1
    return pl.pallas_call(
        functools.partial(update_kernel, z),
        out_shape=jax.ShapeDtypeStruct((CORES, z.G, z.X, z.R, h, n), jnp.float32),
        in_specs=[pl.BlockSpec(memory_space=pl.ANY)],
        out_specs=pl.BlockSpec(memory_space=pl.ANY),
        scratch_shapes=[
            pltpu.VMEM((z.C, h, n), jnp.float32),
            pltpu.VMEM((h, n), jnp.float32),
            pltpu.SemaphoreType.DMA((n_sem,)),
            pltpu.SemaphoreType.DMA((n_sem,)),
            pltpu.SemaphoreType.DMA((1,)),
        ],
        compiler_params=pltpu.CompilerParams(collective_id=1, has_side_effects=True),
        name="exchange_update",
    )(part)


def lifted_kernel(z, part, out, got, total, send, recv, keep):
    g, r, c = here()
    x, core = c // CORES, c % CORES
    h = total.shape[0]
    sems = Sems(send, recv)
    greet(
        [(g, (r + d) % z.R, c) for d in range(1, z.R)]
        + [(g, r, (x + dx) % z.X * CORES + core) for dx in range(1, z.X)]
        + [(g, r, x * CORES + 1 - core)]
    )

    def chunk(k):
        return part.at[pl.ds(pl.multiple_of(k * h, 8), h)]

    own = pltpu.make_async_copy(chunk(r), got.at[r], keep.at[0])
    own.start()
    first = []
    for d in range(1, z.R):
        ss, rs = sems.next()
        t = (r + d) % z.R
        first.append((remote(chunk(t), got.at[r], ss, rs, (g, t, c)), got.at[(r - d + z.R) % z.R], rs))
    own.wait()
    arrive(first)
    acc = got[0]
    for k in range(1, z.R):
        acc = acc + got[k]
    total[...] = acc
    own = pltpu.make_async_copy(total, out.at[core, x, r], keep.at[0])
    own.start()
    second = row_send(z, total, lambda rr: out.at[core, x, rr], sems)
    own.wait()
    arrive(second)
    third = plane_send(z, lambda gg, xx: out.at[core, xx], sems, [(0, dx) for dx in range(1, z.X)])
    arrive(third)
    fourth = core_send(z, lambda a: out.at[a], sems)
    arrive(fourth)
    for w in (first, second, third, fourth):
        sent(w)


def exchange_lifted(z, part):
    n, b1 = part.shape
    h = n // z.R
    n_sem = 2 * z.R + z.X + 1
    return pl.pallas_call(
        functools.partial(lifted_kernel, z),
        out_shape=jax.ShapeDtypeStruct((CORES, z.X, z.R, h, b1), jnp.float32),
        in_specs=[pl.BlockSpec(memory_space=pl.ANY)],
        out_specs=pl.BlockSpec(memory_space=pl.ANY),
        scratch_shapes=[
            pltpu.VMEM((z.R, h, b1), jnp.float32),
            pltpu.VMEM((h, b1), jnp.float32),
            pltpu.SemaphoreType.DMA((n_sem,)),
            pltpu.SemaphoreType.DMA((n_sem,)),
            pltpu.SemaphoreType.DMA((1,)),
        ],
        compiler_params=pltpu.CompilerParams(collective_id=2, has_side_effects=True),
        name="exchange_lifted",
    )(part)


def group_block(GL, k, j):
    idx = k * (k - 1) // 2 + j
    return jnp.concatenate([GL[q, idx] for q in range(GL.shape[0])], axis=0)


def forward_kernel(z, GL, GR, inv, off, y_ref, part_ref):
    b1 = inv.shape[1]
    ys = []
    for k in range(z.R):
        res = GR[k]
        for j in range(k):
            res = res - mm(group_block(GL, k, j), ys[j])
        ys.append(mm(inv[k * b1 : (k + 1) * b1], res))
        y_ref[k * b1 : (k + 1) * b1] = ys[k]
    c = lax.axis_index("col")
    own = y_ref[pl.ds(pl.multiple_of(c * b1, 8), b1)]
    part_ref[...] = mm(off[...], own)


def root_kernel(z, spb, UPD, ROWS, RR, RL, E, own_rows, off, x_ref, lift_ref, side, xt_ref):
    W0, span = E.shape
    p, n = RR.shape[-2:]
    h = UPD.shape[-2]
    b1 = h * z.C
    for g in range(z.G):
        for r in range(z.R):
            for c in range(z.C):
                at = ((g * z.R + r) * z.C + c) * p
                side[at : at + p] = RR[c % CORES, g, c // CORES, r]
    packed = []
    for g in range(z.G):
        u = jnp.concatenate(
            [UPD[c % CORES, g, c // CORES, r] for r in range(z.R) for c in range(z.C)], axis=0
        )
        packed.append(
            (
                jnp.concatenate(split(u), axis=1),
                jnp.concatenate([ROWS[g, r] for r in range(z.R)], axis=1),
            )
        )

    def block(k, j):
        pieces = []
        for s in range(spb):
            idx = spb * (k * (k - 1) // 2) + s * k + j
            pieces += [RL[q, idx] for q in range(RL.shape[0])]
        return jnp.concatenate(pieces, axis=0)

    ys = []
    for k in range(z.C):
        res = side[k * span : (k + 1) * span]
        for w, rows in packed:
            ids = lax.broadcasted_iota(jnp.int32, (span, rows.shape[1]), 0) + k * span
            hot = jnp.where(ids == rows, 1.0, 0.0).astype(jnp.bfloat16)
            both = bdot(hot, w)
            res = res - (both[:, :n] + both[:, n:])
        for j in range(k):
            res = res - mm(block(k, j), ys[j])
        ys.append(mm(E[k * span : (k + 1) * span], res))
    xs = [None] * z.C
    for k in reversed(range(z.C)):
        res = ys[k].T
        for i in range(k + 1, z.C):
            res = res - tmm(xs[i], block(i, k))
        xs[k] = tmm(res, E[k * span : (k + 1) * span])
        side[k * span : (k + 1) * span] = xs[k].T
    g, r, c = here()
    flat = (g * z.R + r) * z.C + c
    x_ref[...] = side[pl.ds(flat * p, p)]
    picked = jnp.zeros((n, b1), jnp.float32)
    for k in range(z.C):
        ids = lax.broadcasted_iota(jnp.int32, (span, b1), 0) + k * span
        hot = jnp.where(ids == own_rows[...], 1.0, 0.0).astype(jnp.bfloat16)
        both = bdot(jnp.concatenate(split(xs[k]), axis=0), hot)
        picked = picked + both[:n] + both[n:]
    lift_ref[...] = tmm(picked, off[...])


def backward_kernel(z, GL, inv, y_ref, lift, out_ref, xs_ref):
    b1 = inv.shape[1]
    xs = [None] * z.R
    for k in reversed(range(z.R)):
        lk = jnp.concatenate([lift[k % CORES, k // CORES, r] for r in range(z.R)], axis=0)
        res = y_ref[k * b1 : (k + 1) * b1].T - lk
        for i in range(k + 1, z.R):
            res = res - tmm(xs[i], group_block(GL, i, k))
        xs[k] = tmm(res, inv[k * b1 : (k + 1) * b1])
        xs_ref[k * b1 : (k + 1) * b1] = xs[k].T
    r = lax.axis_index("row")
    out_ref[...] = xs_ref[pl.ds(pl.multiple_of(r * b1, 8), b1)]


def on_chip(body, out_shape, scratch, name, *args):
    return pl.pallas_call(
        body,
        out_shape=out_shape,
        scratch_shapes=scratch,
        compiler_params=pltpu.CompilerParams(vmem_limit_bytes=VMEM_BYTES),
        name=name,
    )(*args)


def local(z, group_rhs, group_lower, group_diag_inv, group_offdiag, group_rows, root_rhs, root_lower, root_diag_inv):
    f32 = jnp.float32
    b1, n = group_rhs.shape[1:]
    width = group_diag_inv.shape[1]
    W0, span = root_diag_inv.shape
    strip = root_lower.shape[0]
    spb = span // strip
    inv, off = group_diag_inv[0], group_offdiag[0]
    with_root = strip % (8 * z.G * z.C) == 0
    got = gather_all(z, spb, with_root, group_lower[0], group_rhs[0], group_rows, root_rhs, root_lower)
    GL, GR, ROWS, RR = got[:4]
    if with_root:
        RL = got[4].reshape((z.G * z.C,) + got[4].shape[3:])
    else:
        whole = lax.all_gather(root_lower, ("grp", "row", "col"))
        whole = whole.reshape(z.G * z.R, z.C, strip, span)
        RL = jnp.stack(
            [whole[k * spb + s, j] for k in range(z.C) for s in range(spb) for j in range(k)]
        )[None]
    GL = GL.reshape((z.C,) + GL.shape[2:])
    y, part = on_chip(
        functools.partial(forward_kernel, z),
        [jax.ShapeDtypeStruct((width, n), f32), jax.ShapeDtypeStruct((b1, n), f32)],
        [], "group_forward", GL, GR, inv, off,
    )
    UPD = exchange_update(z, part)
    root_x, lift = on_chip(
        functools.partial(root_kernel, z, spb),
        [jax.ShapeDtypeStruct(root_rhs.shape, f32), jax.ShapeDtypeStruct((n, b1), f32)],
        [pltpu.VMEM((W0, n), f32), pltpu.VMEM((n, W0), f32)],
        "root_solve", UPD, ROWS, RR, RL, root_diag_inv, group_rows, off,
    )
    lifted = exchange_lifted(z, lift)
    out = on_chip(
        functools.partial(backward_kernel, z),
        jax.ShapeDtypeStruct((b1, n), f32),
        [pltpu.VMEM((width, n), f32)],
        "group_backward", GL, inv, y, lifted,
    )
    return out[None], root_x


def solution(mesh):
    z = Sizes(mesh.shape)
    placed = (
        P("grp", "row", None),
        P("grp", "row", "col"),
        P("grp", None, None),
        P("grp", "row", "col"),
        P("grp", "row"),
        P(("grp", "row", "col"), None),
        P(("grp", "row"), "col"),
        P(),
    )
    return jax.shard_map(
        functools.partial(local, z),
        mesh=mesh,
        in_specs=placed,
        out_specs=(P("grp", "row", None), P(("grp", "row", "col"), None)),
        check_vma=False,
    )
```

```python
import functools

import jax
import jax.numpy as jnp
from jax import lax
from jax.experimental import pallas as pl
from jax.experimental.pallas import tpu as pltpu
from jax.sharding import PartitionSpec as P

CORES = 2
MESH = pl.DeviceIdType.MESH
VMEM_BYTES = 56 * 1024 * 1024


def split(a):
    high = a.astype(jnp.bfloat16)
    low = (a - high.astype(jnp.float32)).astype(jnp.bfloat16)
    return high, low


def bdot(a, b):
    return jnp.dot(a, b, preferred_element_type=jnp.float32)


def mm(a, b):
    ah, al = split(a)
    n = b.shape[1]
    w = jnp.concatenate(split(b), axis=1)
    both = bdot(ah, w) + bdot(al, w)
    return both[:, :n] + both[:, n:]


def tmm(xt, a):
    ah, al = split(a)
    n = xt.shape[0]
    v = jnp.concatenate(split(xt), axis=0)
    both = bdot(v, ah) + bdot(v, al)
    return both[:n] + both[n:]


class Sizes:
    def __init__(self, mesh_shape):
        self.G, self.R, self.C = mesh_shape["grp"], mesh_shape["row"], mesh_shape["col"]
        self.X = self.C // CORES


def here():
    return lax.axis_index("grp"), lax.axis_index("row"), lax.axis_index("col")


def remote(src, dst, ss, rs, dev):
    cp = pltpu.make_async_remote_copy(
        src_ref=src, dst_ref=dst, send_sem=ss, recv_sem=rs, device_id=dev, device_id_type=MESH
    )
    cp.start()
    return cp


def wait_on(ref, sem):
    pltpu.make_async_copy(ref, ref, sem).wait()


def greet(devs):
    barrier = pltpu.get_barrier_semaphore()
    for dev in devs:
        pl.semaphore_signal(barrier, inc=1, device_id=dev, device_id_type=MESH)
    pl.semaphore_wait(barrier, len(devs))


class Sems:
    def __init__(self, send, recv):
        self.send, self.recv, self.at = send, recv, 0

    def next(self):
        k = self.at
        self.at += 1
        return self.send.at[k], self.recv.at[k]

    def block(self, n):
        self.at += n
        return self.at - n


def plane_offsets(z):
    return [(dg, dx) for dg in range(z.G) for dx in range(z.X) if dg or dx]


def row_send(z, src, slot, sems):
    g, r, c = here()
    waits = []
    for d in range(1, z.R):
        ss, rs = sems.next()
        cp = remote(src, slot(r), ss, rs, (g, (r + d) % z.R, c))
        waits.append((cp, slot((r - d + z.R) % z.R), rs))
    return waits


def plane_send(z, slot, sems, offsets=None):
    g, r, c = here()
    x, core = c // CORES, c % CORES
    waits = []
    for dg, dx in plane_offsets(z) if offsets is None else offsets:
        ss, rs = sems.next()
        tg, tx = (g + dg) % z.G, (x + dx) % z.X
        fg, fx = (g - dg + z.G) % z.G, (x - dx + z.X) % z.X
        cp = remote(slot(g, x), slot(g, x), ss, rs, (tg, r, tx * CORES + core))
        waits.append((cp, slot(fg, fx), rs))
    return waits


def core_send(z, slot, sems):
    g, r, c = here()
    x, core = c // CORES, c % CORES
    ss, rs = sems.next()
    cp = remote(slot(core), slot(core), ss, rs, (g, r, x * CORES + 1 - core))
    return [(cp, slot(1 - core), rs)]


def arrive(waits):
    for _, ref, rs in waits:
        wait_on(ref, rs)


def sent(waits):
    for cp, _, _ in waits:
        cp.wait_send()


def pair_count(n):
    return n * (n - 1) // 2


class Pieces:
    def __init__(self, z, src, slot, held, index, count, groups, forward, sems):
        self.z, self.src, self.slot, self.held, self.index = z, src, slot, held, index
        self.count, self.groups, self.forward = count, groups, forward
        g = lax.axis_index("grp")
        self.gs = range(z.G) if groups else (g,)
        self.sources = [(gs, cs) for gs in self.gs for cs in range(z.C)]
        self.plane = [(dg, dc) for dg in (range(z.G) if groups else (0,)) for dc in range(z.C)]
        self.offs = plane_offsets(z) if forward else []
        ns, no = len(self.sources), len(self.offs)
        self.send, self.recv = sems.send, sems.recv
        self.b_recv = sems.block(count)
        self.b_first = sems.block(len(self.plane))
        self.b_row = sems.block(ns * z.R)
        self.b_on = sems.block(ns * z.R * no)
        self.b_on_recv = sems.block(no * count)

    def mine(self, k):
        g, r, c = here()
        return self.slot(c % CORES, g, c // CORES, k)

    def copies(self, start):
        z = self.z
        g, r, c = here()
        k = self.index(g, r, c)
        rows_each = self.slot(0, 0, 0, 0).shape[0]

        @pl.when(self.held(g, r, c))
        def _():
            for m, (dg, dc) in enumerate(self.plane):
                tg, tc = (g + dg) % z.G, (c + dc) % z.C
                tx, tcore = tc // CORES, tc % CORES
                q = (tcore * z.G + tg) * z.X + tx if self.groups else tcore * z.X + tx
                chunk = self.src.at[pl.ds(pl.multiple_of(q * rows_each, 8), rows_each)]
                dst, rs = self.slot(tcore, tg, tx, k), self.recv.at[self.b_recv + k]
                if dg or dc:
                    cp = pltpu.make_async_remote_copy(
                        src_ref=chunk, dst_ref=dst, send_sem=self.send.at[self.b_first + m],
                        recv_sem=rs, device_id=(tg, r, tc), device_id_type=MESH,
                    )
                    cp.start() if start else cp.wait_send()
                elif start:
                    pltpu.make_async_copy(chunk, dst, rs).start()

    def onward(self, d, start):
        z = self.z
        g, r, c = here()
        x, core = c // CORES, c % CORES
        rs = (r - d + z.R) % z.R
        for m, (gs, cs) in enumerate(self.sources):
            k = self.index(gs, rs, cs)

            @pl.when(self.held(gs, rs, cs))
            def _():
                if start:
                    wait_on(self.mine(k), self.recv.at[self.b_recv + k])
                targets = []
                if d == 0:
                    for e in range(1, z.R):
                        targets.append(
                            ((g, (r + e) % z.R, c), self.b_row + m * z.R + e, self.b_recv + k)
                        )
                for o, (dg, dx) in enumerate(self.offs):
                    targets.append(
                        (
                            ((g + dg) % z.G, r, (x + dx) % z.X * CORES + core),
                            self.b_on + (d * len(self.sources) + m) * len(self.offs) + o,
                            self.b_on_recv + o * self.count + k,
                        )
                    )
                for dev, si, ri in targets:
                    cp = pltpu.make_async_remote_copy(
                        src_ref=self.mine(k), dst_ref=self.mine(k), send_sem=self.send.at[si],
                        recv_sem=self.recv.at[ri], device_id=dev, device_id_type=MESH,
                    )
                    cp.start() if start else cp.wait_send()

    def plane_arrived(self, o):
        z = self.z
        g, r, c = here()
        x, core = c // CORES, c % CORES
        dg, dx = self.offs[o]
        fg, fx = (g - dg + z.G) % z.G, (x - dx + z.X) % z.X
        for k in range(self.count):
            wait_on(self.slot(core, fg, fx, k), self.recv.at[self.b_on_recv + o * self.count + k])
        return fg, fx

    def finish(self):
        self.copies(False)
        for d in range(self.z.R):
            self.onward(d, False)


def gather_kernel(z, spb, with_root, refs_in, refs_out, GL, GR, part, got, total, send, recv, keep):
    g, r, c = here()
    x, core = c // CORES, c % CORES
    glow, grhs, rows, rrhs, inv, off = refs_in[:6]
    GL_out, ROWS, RR, y_ref, UPD = refs_out[:5]
    sems = Sems(send, recv)
    groups = range(z.G) if with_root else (0,)
    devs = [
        ((g + dg) % z.G, r, (c + dc) % z.C) for dg in groups for dc in range(z.C) if dg or dc
    ] + [(g, (r + d) % z.R, c) for d in range(1, z.R)]
    if not with_root:
        devs += [
            ((g + dg) % z.G, r, (x + dx) % z.X * CORES + core)
            for dg, dx in plane_offsets(z) if dg
        ]
    greet(devs)

    low = Pieces(
        z, glow, lambda a, b, d, k: GL.at[a, d, k], lambda gg, rr, cc: cc < rr,
        lambda gg, rr, cc: rr * (rr - 1) // 2 + cc, pair_count(z.R), False, False, sems,
    )
    low.copies(True)
    if with_root:
        rlow, RL = refs_in[6], refs_out[5]

        def index(gg, rr, cc):
            strip = gg * z.R + rr
            kb = strip // spb
            return spb * (kb * (kb - 1) // 2) + (strip - kb * spb) * kb + cc

        root = Pieces(
            z, rlow, lambda a, b, d, k: RL.at[a, b, d, k],
            lambda gg, rr, cc: cc < (gg * z.R + rr) // spb,
            index, spb * pair_count(z.C), True, True, sems,
        )
        root.copies(True)
    locals_ = []
    for k, (src, dst) in enumerate(
        ((grhs, GR.at[r]), (rows, ROWS.at[g, r]), (rrhs, RR.at[core, g, x, r]))
    ):
        cp = pltpu.make_async_copy(src, dst, keep.at[k])
        cp.start()
        locals_.append(cp)
    rhs_w = row_send(z, grhs, lambda rr: GR.at[rr], sems)
    rows_w = row_send(z, rows, lambda rr: ROWS.at[g, rr], sems)
    rr_w = row_send(z, rrhs, lambda rr: RR.at[core, g, x, rr], sems)
    low.onward(0, True)
    if with_root:
        root.onward(0, True)
    for cp in locals_:
        cp.wait()
    arrive(rows_w)
    rows_p = []
    for dg in range(1, z.G):
        ss, rs = sems.next()
        cp = remote(ROWS.at[g], ROWS.at[g], ss, rs, ((g + dg) % z.G, r, c))
        rows_p.append((cp, ROWS.at[(g - dg + z.G) % z.G], rs))
    arrive(rr_w)
    rr_p = plane_send(z, lambda gg, xx: RR.at[core, gg, xx], sems)
    for d in range(1, z.R):
        low.onward(d, True)
    gl_p = plane_send(
        z, lambda gg, xx: GL.at[core, xx], sems, [(0, dx) for dx in range(1, z.X)]
    )
    if with_root:
        for d in range(1, z.R):
            root.onward(d, True)
    arrive(rr_p)
    rr_c = core_send(z, lambda a: RR.at[a], sems)
    arrive(gl_p)
    gl_c = core_send(z, lambda a: GL.at[a], sems)
    pending = [rhs_w, rows_w, rr_w, rows_p, rr_p, gl_p, rr_c, gl_c]
    late = [rows_p, rr_c]
    if with_root:
        rl_c = core_send(z, lambda a: RL.at[a, g, x], sems)
    arrive(rhs_w)
    arrive(gl_c)
    copy_out = pltpu.make_async_copy(GL, GL_out, keep.at[3])
    copy_out.start()
    forward(z, GL, GR, inv, off, y_ref, part)

    h = total.shape[0]

    def chunk(k):
        return part.at[pl.ds(pl.multiple_of(k * h, 8), h)]

    own = pltpu.make_async_copy(chunk(c), got.at[c], keep.at[0])
    own.start()
    first = []
    for d in range(1, z.C):
        ss, rs = sems.next()
        t = (c + d) % z.C
        first.append((remote(chunk(t), got.at[c], ss, rs, (g, r, t)), got.at[(c - d + z.C) % z.C], rs))
    own.wait()
    arrive(first)
    acc = got[0]
    for k in range(1, z.C):
        acc = acc + got[k]
    total[...] = acc
    own = pltpu.make_async_copy(total, UPD.at[core, g, x, r], keep.at[0])
    own.start()
    second = row_send(z, total, lambda rr: UPD.at[core, g, x, rr], sems)
    own.wait()
    arrive(second)
    third = plane_send(z, lambda gg, xx: UPD.at[core, gg, xx], sems)
    if with_root:
        for o in range(len(root.offs)):
            fg, fx = root.plane_arrived(o)
            rl_c += core_send(z, lambda a: RL.at[a, fg, fx], sems)
        pending += [rl_c]
        late += [rl_c]
    arrive(third)
    fourth = core_send(z, lambda a: UPD.at[a], sems)
    late += [fourth]
    pending += [first, second, third, fourth]
    for w in late:
        arrive(w)
    for w in pending:
        sent(w)
    copy_out.wait()
    low.finish()
    if with_root:
        root.finish()


def gather_all(z, spb, with_root, glow, grhs, rows, rrhs, inv, off, rlow):
    f32 = jnp.float32
    b1, n = grhs.shape
    ins = [glow, grhs, rows, rrhs, inv, off] + ([rlow] if with_root else [])
    outs = [
        jax.ShapeDtypeStruct((CORES, z.X, pair_count(z.R), b1 // z.C, b1), f32),
        jax.ShapeDtypeStruct((z.G, z.R, 1, b1), jnp.int32),
        jax.ShapeDtypeStruct((CORES, z.G, z.X, z.R) + rrhs.shape, f32),
        jax.ShapeDtypeStruct((z.R * b1, n), f32),
        jax.ShapeDtypeStruct((CORES, z.G, z.X, z.R, b1 // z.C, n), f32),
    ]
    if with_root:
        s, span = rlow.shape
        outs.append(
            jax.ShapeDtypeStruct(
                (CORES, z.G, z.X, spb * pair_count(z.C), s // (z.G * z.C), span), f32
            )
        )
    n_in, n_out = len(ins), len(outs)
    n_sem = 5 * z.R + 3 * z.G * z.X + z.X + z.G + z.C + 5
    n_sem += pair_count(z.R) + z.C + z.C * z.R
    if with_root:
        count, ns, no = spb * pair_count(z.C), z.G * z.C, z.G * z.X - 1
        n_sem += count + ns + ns * z.R + ns * z.R * no + no * count + z.G * z.X

    def body(*refs):
        gather_kernel(z, spb, with_root, refs[:n_in], refs[n_in : n_in + n_out], *refs[n_in + n_out :])

    return pl.pallas_call(
        body,
        out_shape=outs,
        in_specs=[
            pl.BlockSpec(memory_space=pltpu.VMEM if k in (4, 5) else pl.ANY) for k in range(n_in)
        ],
        out_specs=[
            pl.BlockSpec(memory_space=pltpu.VMEM if k == 3 else pl.ANY) for k in range(n_out)
        ],
        scratch_shapes=[
            pltpu.VMEM(outs[0].shape, f32),
            pltpu.VMEM((z.R, b1, n), f32),
            pltpu.VMEM((b1, n), f32),
            pltpu.VMEM((z.C, b1 // z.C, n), f32),
            pltpu.VMEM((b1 // z.C, n), f32),
            pltpu.SemaphoreType.DMA((n_sem,)),
            pltpu.SemaphoreType.DMA((n_sem,)),
            pltpu.SemaphoreType.DMA((4,)),
        ],
        compiler_params=pltpu.CompilerParams(
            collective_id=0, has_side_effects=True, vmem_limit_bytes=VMEM_BYTES // 2
        ),
        name="gather_factors",
    )(*ins)


def lifted_kernel(z, part, out, got, total, send, recv, keep):
    g, r, c = here()
    x, core = c // CORES, c % CORES
    h = total.shape[0]
    sems = Sems(send, recv)
    greet(
        [(g, (r + d) % z.R, c) for d in range(1, z.R)]
        + [(g, r, (x + dx) % z.X * CORES + core) for dx in range(1, z.X)]
        + [(g, r, x * CORES + 1 - core)]
    )

    def chunk(k):
        return part.at[pl.ds(pl.multiple_of(k * h, 8), h)]

    own = pltpu.make_async_copy(chunk(r), got.at[r], keep.at[0])
    own.start()
    first = []
    for d in range(1, z.R):
        ss, rs = sems.next()
        t = (r + d) % z.R
        first.append((remote(chunk(t), got.at[r], ss, rs, (g, t, c)), got.at[(r - d + z.R) % z.R], rs))
    own.wait()
    arrive(first)
    acc = got[0]
    for k in range(1, z.R):
        acc = acc + got[k]
    total[...] = acc
    own = pltpu.make_async_copy(total, out.at[core, x, r], keep.at[0])
    own.start()
    second = row_send(z, total, lambda rr: out.at[core, x, rr], sems)
    own.wait()
    arrive(second)
    third = plane_send(z, lambda gg, xx: out.at[core, xx], sems, [(0, dx) for dx in range(1, z.X)])
    arrive(third)
    fourth = core_send(z, lambda a: out.at[a], sems)
    arrive(fourth)
    for w in (first, second, third, fourth):
        sent(w)


def exchange_lifted(z, part):
    n, b1 = part.shape
    h = n // z.R
    n_sem = 2 * z.R + z.X + 1
    return pl.pallas_call(
        functools.partial(lifted_kernel, z),
        out_shape=jax.ShapeDtypeStruct((CORES, z.X, z.R, h, b1), jnp.float32),
        in_specs=[pl.BlockSpec(memory_space=pl.ANY)],
        out_specs=pl.BlockSpec(memory_space=pl.ANY),
        scratch_shapes=[
            pltpu.VMEM((z.R, h, b1), jnp.float32),
            pltpu.VMEM((h, b1), jnp.float32),
            pltpu.SemaphoreType.DMA((n_sem,)),
            pltpu.SemaphoreType.DMA((n_sem,)),
            pltpu.SemaphoreType.DMA((1,)),
        ],
        compiler_params=pltpu.CompilerParams(collective_id=2, has_side_effects=True),
        name="exchange_lifted",
    )(part)


def group_block(GL, k, j):
    idx = k * (k - 1) // 2 + j
    return jnp.concatenate([GL[q, idx] for q in range(GL.shape[0])], axis=0)


def forward(z, GL, GR, inv, off, y_ref, part_ref):
    b1 = inv.shape[1]
    ys = []
    for k in range(z.R):
        res = GR[k]
        for j in range(k):
            idx = k * (k - 1) // 2 + j
            low = jnp.concatenate(
                [GL[core, x, idx] for core in range(CORES) for x in range(z.X)], axis=0
            )
            res = res - mm(low, ys[j])
        ys.append(mm(inv[k * b1 : (k + 1) * b1], res))
        y_ref[k * b1 : (k + 1) * b1] = ys[k]
    c = lax.axis_index("col")
    own = y_ref[pl.ds(pl.multiple_of(c * b1, 8), b1)]
    part_ref[...] = mm(off[...], own)


def root_kernel(z, spb, UPD, ROWS, RR, RL, E, own_rows, off, x_ref, lift_ref, side, xt_ref):
    W0, span = E.shape
    p, n = RR.shape[-2:]
    h = UPD.shape[-2]
    b1 = h * z.C
    for g in range(z.G):
        for r in range(z.R):
            for c in range(z.C):
                at = ((g * z.R + r) * z.C + c) * p
                side[at : at + p] = RR[c % CORES, g, c // CORES, r]
    packed = []
    for g in range(z.G):
        u = jnp.concatenate(
            [UPD[c % CORES, g, c // CORES, r] for r in range(z.R) for c in range(z.C)], axis=0
        )
        packed.append(
            (
                jnp.concatenate(split(u), axis=1),
                jnp.concatenate([ROWS[g, r] for r in range(z.R)], axis=1),
            )
        )

    def block(k, j):
        pieces = []
        for s in range(spb):
            idx = spb * (k * (k - 1) // 2) + s * k + j
            pieces += [RL[q, idx] for q in range(RL.shape[0])]
        return jnp.concatenate(pieces, axis=0)

    ys = []
    for k in range(z.C):
        res = side[k * span : (k + 1) * span]
        for w, rows in packed:
            ids = lax.broadcasted_iota(jnp.int32, (span, rows.shape[1]), 0) + k * span
            hot = jnp.where(ids == rows, 1.0, 0.0).astype(jnp.bfloat16)
            both = bdot(hot, w)
            res = res - (both[:, :n] + both[:, n:])
        for j in range(k):
            res = res - mm(block(k, j), ys[j])
        ys.append(mm(E[k * span : (k + 1) * span], res))
    xs = [None] * z.C
    for k in reversed(range(z.C)):
        res = ys[k].T
        for i in range(k + 1, z.C):
            res = res - tmm(xs[i], block(i, k))
        xs[k] = tmm(res, E[k * span : (k + 1) * span])
        side[k * span : (k + 1) * span] = xs[k].T
    g, r, c = here()
    flat = (g * z.R + r) * z.C + c
    x_ref[...] = side[pl.ds(flat * p, p)]
    picked = jnp.zeros((n, b1), jnp.float32)
    for k in range(z.C):
        ids = lax.broadcasted_iota(jnp.int32, (span, b1), 0) + k * span
        hot = jnp.where(ids == own_rows[...], 1.0, 0.0).astype(jnp.bfloat16)
        both = bdot(jnp.concatenate(split(xs[k]), axis=0), hot)
        picked = picked + both[:n] + both[n:]
    lift_ref[...] = tmm(picked, off[...])


def backward_kernel(z, GL, inv, y_ref, lift, out_ref, xs_ref):
    b1 = inv.shape[1]
    xs = [None] * z.R
    for k in reversed(range(z.R)):
        lk = jnp.concatenate([lift[k % CORES, k // CORES, r] for r in range(z.R)], axis=0)
        res = y_ref[k * b1 : (k + 1) * b1].T - lk
        for i in range(k + 1, z.R):
            res = res - tmm(xs[i], group_block(GL, i, k))
        xs[k] = tmm(res, inv[k * b1 : (k + 1) * b1])
        xs_ref[k * b1 : (k + 1) * b1] = xs[k].T
    r = lax.axis_index("row")
    out_ref[...] = xs_ref[pl.ds(pl.multiple_of(r * b1, 8), b1)]


def on_chip(body, out_shape, scratch, name, *args):
    return pl.pallas_call(
        body,
        out_shape=out_shape,
        scratch_shapes=scratch,
        compiler_params=pltpu.CompilerParams(vmem_limit_bytes=VMEM_BYTES),
        name=name,
    )(*args)


def local(z, group_rhs, group_lower, group_diag_inv, group_offdiag, group_rows, root_rhs, root_lower, root_diag_inv):
    f32 = jnp.float32
    b1, n = group_rhs.shape[1:]
    width = group_diag_inv.shape[1]
    W0, span = root_diag_inv.shape
    strip = root_lower.shape[0]
    spb = span // strip
    inv, off = group_diag_inv[0], group_offdiag[0]
    with_root = strip % (8 * z.G * z.C) == 0
    got = gather_all(
        z, spb, with_root, group_lower[0], group_rhs[0], group_rows, root_rhs, inv, off, root_lower
    )
    GL, ROWS, RR, y, UPD = got[:5]
    if with_root:
        RL = got[5].reshape((z.G * z.C,) + got[5].shape[3:])
    else:
        whole = lax.all_gather(root_lower, ("grp", "row", "col"))
        whole = whole.reshape(z.G * z.R, z.C, strip, span)
        RL = jnp.stack(
            [whole[k * spb + s, j] for k in range(z.C) for s in range(spb) for j in range(k)]
        )[None]
    GL = GL.reshape((z.C,) + GL.shape[2:])
    root_x, lift = on_chip(
        functools.partial(root_kernel, z, spb),
        [jax.ShapeDtypeStruct(root_rhs.shape, f32), jax.ShapeDtypeStruct((n, b1), f32)],
        [pltpu.VMEM((W0, n), f32), pltpu.VMEM((n, W0), f32)],
        "root_solve", UPD, ROWS, RR, RL, root_diag_inv, group_rows, off,
    )
    lifted = exchange_lifted(z, lift)
    out = on_chip(
        functools.partial(backward_kernel, z),
        jax.ShapeDtypeStruct((b1, n), f32),
        [pltpu.VMEM((width, n), f32)],
        "group_backward", GL, inv, y, lifted,
    )
    return out[None], root_x


def solution(mesh):
    z = Sizes(mesh.shape)
    placed = (
        P("grp", "row", None),
        P("grp", "row", "col"),
        P("grp", None, None),
        P("grp", "row", "col"),
        P("grp", "row"),
        P(("grp", "row", "col"), None),
        P(("grp", "row"), "col"),
        P(),
    )
    return jax.shard_map(
        functools.partial(local, z),
        mesh=mesh,
        in_specs=placed,
        out_specs=(P("grp", "row", None), P(("grp", "row", "col"), None)),
        check_vma=False,
    )
```

```python
import functools

import jax
import jax.numpy as jnp
from jax import lax
from jax.experimental import pallas as pl
from jax.experimental.pallas import tpu as pltpu
from jax.sharding import PartitionSpec as P

CORES = 2
MESH = pl.DeviceIdType.MESH
VMEM_BYTES = 56 * 1024 * 1024


def split(a):
    high = a.astype(jnp.bfloat16)
    low = (a - high.astype(jnp.float32)).astype(jnp.bfloat16)
    return high, low


def bdot(a, b):
    return jnp.dot(a, b, preferred_element_type=jnp.float32)


def mm(a, b):
    ah, al = split(a)
    n = b.shape[1]
    w = jnp.concatenate(split(b), axis=1)
    both = bdot(ah, w) + bdot(al, w)
    return both[:, :n] + both[:, n:]


def tmm(xt, a):
    ah, al = split(a)
    n = xt.shape[0]
    v = jnp.concatenate(split(xt), axis=0)
    both = bdot(v, ah) + bdot(v, al)
    return both[:n] + both[n:]


class Sizes:
    def __init__(self, mesh_shape):
        self.G, self.R, self.C = mesh_shape["grp"], mesh_shape["row"], mesh_shape["col"]
        self.X = self.C // CORES


def here():
    return lax.axis_index("grp"), lax.axis_index("row"), lax.axis_index("col")


def remote(src, dst, ss, rs, dev):
    cp = pltpu.make_async_remote_copy(
        src_ref=src, dst_ref=dst, send_sem=ss, recv_sem=rs, device_id=dev, device_id_type=MESH
    )
    cp.start()
    return cp


def wait_on(ref, sem):
    pltpu.make_async_copy(ref, ref, sem).wait()


def greet(devs):
    barrier = pltpu.get_barrier_semaphore()
    for dev in devs:
        pl.semaphore_signal(barrier, inc=1, device_id=dev, device_id_type=MESH)
    pl.semaphore_wait(barrier, len(devs))


class Sems:
    def __init__(self, send, recv):
        self.send, self.recv, self.at = send, recv, 0

    def next(self):
        k = self.at
        self.at += 1
        return self.send.at[k], self.recv.at[k]

    def block(self, n):
        self.at += n
        return self.at - n


def plane_offsets(z):
    return [(dg, dx) for dg in range(z.G) for dx in range(z.X) if dg or dx]


def row_send(z, src, slot, sems):
    g, r, c = here()
    waits = []
    for d in range(1, z.R):
        ss, rs = sems.next()
        cp = remote(src, slot(r), ss, rs, (g, (r + d) % z.R, c))
        waits.append((cp, slot((r - d + z.R) % z.R), rs))
    return waits


def plane_send(z, slot, sems, offsets=None):
    g, r, c = here()
    x, core = c // CORES, c % CORES
    waits = []
    for dg, dx in plane_offsets(z) if offsets is None else offsets:
        ss, rs = sems.next()
        tg, tx = (g + dg) % z.G, (x + dx) % z.X
        fg, fx = (g - dg + z.G) % z.G, (x - dx + z.X) % z.X
        cp = remote(slot(g, x), slot(g, x), ss, rs, (tg, r, tx * CORES + core))
        waits.append((cp, slot(fg, fx), rs))
    return waits


def core_send(z, slot, sems):
    g, r, c = here()
    x, core = c // CORES, c % CORES
    ss, rs = sems.next()
    cp = remote(slot(core), slot(core), ss, rs, (g, r, x * CORES + 1 - core))
    return [(cp, slot(1 - core), rs)]


def arrive(waits):
    for _, ref, rs in waits:
        wait_on(ref, rs)


def sent(waits):
    for cp, _, _ in waits:
        cp.wait_send()


def pair_count(n):
    return n * (n - 1) // 2


class Pieces:
    def __init__(self, z, src, slot, held, index, count, groups, forward, sems):
        self.z, self.src, self.slot, self.held, self.index = z, src, slot, held, index
        self.count, self.groups, self.forward = count, groups, forward
        g = lax.axis_index("grp")
        self.gs = range(z.G) if groups else (g,)
        self.sources = [(gs, cs) for gs in self.gs for cs in range(z.C)]
        self.plane = [(dg, dc) for dg in (range(z.G) if groups else (0,)) for dc in range(z.C)]
        self.offs = plane_offsets(z) if forward else []
        ns, no = len(self.sources), len(self.offs)
        self.send, self.recv = sems.send, sems.recv
        self.b_recv = sems.block(count)
        self.b_first = sems.block(len(self.plane))
        self.b_row = sems.block(ns * z.R)
        self.b_on = sems.block(ns * z.R * no)
        self.b_on_recv = sems.block(no * count)

    def mine(self, k):
        g, r, c = here()
        return self.slot(c % CORES, g, c // CORES, k)

    def copies(self, start):
        z = self.z
        g, r, c = here()
        k = self.index(g, r, c)
        rows_each = self.slot(0, 0, 0, 0).shape[0]

        @pl.when(self.held(g, r, c))
        def _():
            for m, (dg, dc) in enumerate(self.plane):
                tg, tc = (g + dg) % z.G, (c + dc) % z.C
                tx, tcore = tc // CORES, tc % CORES
                q = (tcore * z.G + tg) * z.X + tx if self.groups else tcore * z.X + tx
                chunk = self.src.at[pl.ds(pl.multiple_of(q * rows_each, 8), rows_each)]
                dst, rs = self.slot(tcore, tg, tx, k), self.recv.at[self.b_recv + k]
                if dg or dc:
                    cp = pltpu.make_async_remote_copy(
                        src_ref=chunk, dst_ref=dst, send_sem=self.send.at[self.b_first + m],
                        recv_sem=rs, device_id=(tg, r, tc), device_id_type=MESH,
                    )
                    cp.start() if start else cp.wait_send()
                elif start:
                    pltpu.make_async_copy(chunk, dst, rs).start()

    def onward(self, d, start):
        z = self.z
        g, r, c = here()
        x, core = c // CORES, c % CORES
        rs = (r - d + z.R) % z.R
        for m, (gs, cs) in enumerate(self.sources):
            k = self.index(gs, rs, cs)

            @pl.when(self.held(gs, rs, cs))
            def _():
                if start:
                    wait_on(self.mine(k), self.recv.at[self.b_recv + k])
                targets = []
                if d == 0:
                    for e in range(1, z.R):
                        targets.append(
                            ((g, (r + e) % z.R, c), self.b_row + m * z.R + e, self.b_recv + k)
                        )
                for o, (dg, dx) in enumerate(self.offs):
                    targets.append(
                        (
                            ((g + dg) % z.G, r, (x + dx) % z.X * CORES + core),
                            self.b_on + (d * len(self.sources) + m) * len(self.offs) + o,
                            self.b_on_recv + o * self.count + k,
                        )
                    )
                for dev, si, ri in targets:
                    cp = pltpu.make_async_remote_copy(
                        src_ref=self.mine(k), dst_ref=self.mine(k), send_sem=self.send.at[si],
                        recv_sem=self.recv.at[ri], device_id=dev, device_id_type=MESH,
                    )
                    cp.start() if start else cp.wait_send()

    def plane_arrived(self, o):
        z = self.z
        g, r, c = here()
        x, core = c // CORES, c % CORES
        dg, dx = self.offs[o]
        fg, fx = (g - dg + z.G) % z.G, (x - dx + z.X) % z.X
        for k in range(self.count):
            wait_on(self.slot(core, fg, fx, k), self.recv.at[self.b_on_recv + o * self.count + k])
        return fg, fx

    def finish(self):
        self.copies(False)
        for d in range(self.z.R):
            self.onward(d, False)


def gather_kernel(z, spb, with_root, refs_in, refs_out, GL, GR, part, got, total, send, recv, keep):
    g, r, c = here()
    x, core = c // CORES, c % CORES
    glow, grhs, rows, rrhs, inv, off = refs_in[:6]
    GL_out, ROWS, RR, y_ref, UPD = refs_out[:5]
    sems = Sems(send, recv)
    groups = range(z.G) if with_root else (0,)
    devs = [
        ((g + dg) % z.G, r, (c + dc) % z.C) for dg in groups for dc in range(z.C) if dg or dc
    ] + [(g, (r + d) % z.R, c) for d in range(1, z.R)]
    if not with_root:
        devs += [
            ((g + dg) % z.G, r, (x + dx) % z.X * CORES + core)
            for dg, dx in plane_offsets(z) if dg
        ]
    greet(devs)

    low = Pieces(
        z, glow, lambda a, b, d, k: GL.at[a, d, k], lambda gg, rr, cc: cc < rr,
        lambda gg, rr, cc: rr * (rr - 1) // 2 + cc, pair_count(z.R), False, False, sems,
    )
    low.copies(True)
    if with_root:
        rlow, RL = refs_in[6], refs_out[5]

        def index(gg, rr, cc):
            strip = gg * z.R + rr
            kb = strip // spb
            return spb * (kb * (kb - 1) // 2) + (strip - kb * spb) * kb + cc

        root = Pieces(
            z, rlow, lambda a, b, d, k: RL.at[a, b, d, k],
            lambda gg, rr, cc: cc < (gg * z.R + rr) // spb,
            index, spb * pair_count(z.C), True, True, sems,
        )
        root.copies(True)
    locals_ = []
    for k, (src, dst) in enumerate(
        ((grhs, GR.at[r]), (rows, ROWS.at[g, r]), (rrhs, RR.at[core, g, x, r]))
    ):
        cp = pltpu.make_async_copy(src, dst, keep.at[k])
        cp.start()
        locals_.append(cp)
    rhs_w = row_send(z, grhs, lambda rr: GR.at[rr], sems)
    rows_w = row_send(z, rows, lambda rr: ROWS.at[g, rr], sems)
    rr_w = row_send(z, rrhs, lambda rr: RR.at[core, g, x, rr], sems)
    low.onward(0, True)
    if with_root:
        root.onward(0, True)
    for cp in locals_:
        cp.wait()
    arrive(rows_w)
    rows_p = []
    for dg in range(1, z.G):
        ss, rs = sems.next()
        cp = remote(ROWS.at[g], ROWS.at[g], ss, rs, ((g + dg) % z.G, r, c))
        rows_p.append((cp, ROWS.at[(g - dg + z.G) % z.G], rs))
    arrive(rr_w)
    rr_p = plane_send(z, lambda gg, xx: RR.at[core, gg, xx], sems)
    for d in range(1, z.R):
        low.onward(d, True)
    gl_p = plane_send(
        z, lambda gg, xx: GL.at[core, xx], sems, [(0, dx) for dx in range(1, z.X)]
    )
    if with_root:
        for d in range(1, z.R):
            root.onward(d, True)
    arrive(rr_p)
    rr_c = core_send(z, lambda a: RR.at[a], sems)
    arrive(gl_p)
    gl_c = core_send(z, lambda a: GL.at[a], sems)
    pending = [rhs_w, rows_w, rr_w, rows_p, rr_p, gl_p, rr_c, gl_c]
    late = [rows_p, rr_c]
    if with_root:
        rl_c = core_send(z, lambda a: RL.at[a, g, x], sems)
    arrive(rhs_w)
    arrive(gl_c)
    copy_out = pltpu.make_async_copy(GL, GL_out, keep.at[3])
    copy_out.start()
    forward(z, GL, GR, inv, off, y_ref, part)

    h = total.shape[0]

    def chunk(k):
        return part.at[pl.ds(pl.multiple_of(k * h, 8), h)]

    own = pltpu.make_async_copy(chunk(c), got.at[c], keep.at[0])
    own.start()
    first = []
    for d in range(1, z.C):
        ss, rs = sems.next()
        t = (c + d) % z.C
        first.append((remote(chunk(t), got.at[c], ss, rs, (g, r, t)), got.at[(c - d + z.C) % z.C], rs))
    own.wait()
    arrive(first)
    acc = got[0]
    for k in range(1, z.C):
        acc = acc + got[k]
    total[...] = acc
    own = pltpu.make_async_copy(total, UPD.at[core, g, x, r], keep.at[0])
    own.start()
    second = row_send(z, total, lambda rr: UPD.at[core, g, x, rr], sems)
    own.wait()
    arrive(second)
    third = plane_send(z, lambda gg, xx: UPD.at[core, gg, xx], sems)
    if with_root:
        for o in range(len(root.offs)):
            fg, fx = root.plane_arrived(o)
            rl_c += core_send(z, lambda a: RL.at[a, fg, fx], sems)
        pending += [rl_c]
        late += [rl_c]
    arrive(third)
    fourth = core_send(z, lambda a: UPD.at[a], sems)
    late += [fourth]
    pending += [first, second, third, fourth]
    for w in late:
        arrive(w)
    for w in pending:
        sent(w)
    copy_out.wait()
    low.finish()
    if with_root:
        root.finish()


def gather_all(z, spb, with_root, glow, grhs, rows, rrhs, inv, off, rlow):
    f32 = jnp.float32
    b1, n = grhs.shape
    ins = [glow, grhs, rows, rrhs, inv, off] + ([rlow] if with_root else [])
    outs = [
        jax.ShapeDtypeStruct((CORES, z.X, pair_count(z.R), b1 // z.C, b1), f32),
        jax.ShapeDtypeStruct((z.G, z.R, 1, b1), jnp.int32),
        jax.ShapeDtypeStruct((CORES, z.G, z.X, z.R) + rrhs.shape, f32),
        jax.ShapeDtypeStruct((z.R * b1, n), f32),
        jax.ShapeDtypeStruct((CORES, z.G, z.X, z.R, b1 // z.C, n), f32),
    ]
    if with_root:
        s, span = rlow.shape
        outs.append(
            jax.ShapeDtypeStruct(
                (CORES, z.G, z.X, spb * pair_count(z.C), s // (z.G * z.C), span), f32
            )
        )
    n_in, n_out = len(ins), len(outs)
    n_sem = 5 * z.R + 3 * z.G * z.X + z.X + z.G + z.C + 5
    n_sem += pair_count(z.R) + z.C + z.C * z.R
    if with_root:
        count, ns, no = spb * pair_count(z.C), z.G * z.C, z.G * z.X - 1
        n_sem += count + ns + ns * z.R + ns * z.R * no + no * count + z.G * z.X

    def body(*refs):
        gather_kernel(z, spb, with_root, refs[:n_in], refs[n_in : n_in + n_out], *refs[n_in + n_out :])

    return pl.pallas_call(
        body,
        out_shape=outs,
        in_specs=[
            pl.BlockSpec(memory_space=pltpu.VMEM if k in (4, 5) else pl.ANY) for k in range(n_in)
        ],
        out_specs=[
            pl.BlockSpec(memory_space=pltpu.VMEM if k == 3 else pl.ANY) for k in range(n_out)
        ],
        scratch_shapes=[
            pltpu.VMEM(outs[0].shape, f32),
            pltpu.VMEM((z.R, b1, n), f32),
            pltpu.VMEM((b1, n), f32),
            pltpu.VMEM((z.C, b1 // z.C, n), f32),
            pltpu.VMEM((b1 // z.C, n), f32),
            pltpu.SemaphoreType.DMA((n_sem,)),
            pltpu.SemaphoreType.DMA((n_sem,)),
            pltpu.SemaphoreType.DMA((4,)),
        ],
        compiler_params=pltpu.CompilerParams(
            collective_id=0, has_side_effects=True, vmem_limit_bytes=VMEM_BYTES
        ),
        name="gather_factors",
    )(*ins)


def lifted_kernel(z, part, out, got, total, send, recv, keep):
    g, r, c = here()
    x, core = c // CORES, c % CORES
    h = total.shape[0]
    sems = Sems(send, recv)
    greet(
        [(g, (r + d) % z.R, c) for d in range(1, z.R)]
        + [(g, r, (x + dx) % z.X * CORES + core) for dx in range(1, z.X)]
        + [(g, r, x * CORES + 1 - core)]
    )

    def chunk(k):
        return part.at[pl.ds(pl.multiple_of(k * h, 8), h)]

    own = pltpu.make_async_copy(chunk(r), got.at[r], keep.at[0])
    own.start()
    first = []
    for d in range(1, z.R):
        ss, rs = sems.next()
        t = (r + d) % z.R
        first.append((remote(chunk(t), got.at[r], ss, rs, (g, t, c)), got.at[(r - d + z.R) % z.R], rs))
    own.wait()
    arrive(first)
    acc = got[0]
    for k in range(1, z.R):
        acc = acc + got[k]
    total[...] = acc
    own = pltpu.make_async_copy(total, out.at[core, x, r], keep.at[0])
    own.start()
    second = row_send(z, total, lambda rr: out.at[core, x, rr], sems)
    own.wait()
    arrive(second)
    third = plane_send(z, lambda gg, xx: out.at[core, xx], sems, [(0, dx) for dx in range(1, z.X)])
    arrive(third)
    fourth = core_send(z, lambda a: out.at[a], sems)
    arrive(fourth)
    for w in (first, second, third, fourth):
        sent(w)


def exchange_lifted(z, part):
    n, b1 = part.shape
    h = n // z.R
    n_sem = 2 * z.R + z.X + 1
    return pl.pallas_call(
        functools.partial(lifted_kernel, z),
        out_shape=jax.ShapeDtypeStruct((CORES, z.X, z.R, h, b1), jnp.float32),
        in_specs=[pl.BlockSpec(memory_space=pl.ANY)],
        out_specs=pl.BlockSpec(memory_space=pl.ANY),
        scratch_shapes=[
            pltpu.VMEM((z.R, h, b1), jnp.float32),
            pltpu.VMEM((h, b1), jnp.float32),
            pltpu.SemaphoreType.DMA((n_sem,)),
            pltpu.SemaphoreType.DMA((n_sem,)),
            pltpu.SemaphoreType.DMA((1,)),
        ],
        compiler_params=pltpu.CompilerParams(collective_id=2, has_side_effects=True),
        name="exchange_lifted",
    )(part)


def group_block(GL, k, j):
    idx = k * (k - 1) // 2 + j
    return jnp.concatenate([GL[q, idx] for q in range(GL.shape[0])], axis=0)


def forward(z, GL, GR, inv, off, y_ref, part_ref):
    b1 = inv.shape[1]
    ys = []
    for k in range(z.R):
        res = GR[k]
        for j in range(k):
            idx = k * (k - 1) // 2 + j
            low = jnp.concatenate(
                [GL[core, x, idx] for core in range(CORES) for x in range(z.X)], axis=0
            )
            res = res - mm(low, ys[j])
        ys.append(mm(inv[k * b1 : (k + 1) * b1], res))
        y_ref[k * b1 : (k + 1) * b1] = ys[k]
    c = lax.axis_index("col")
    own = y_ref[pl.ds(pl.multiple_of(c * b1, 8), b1)]
    part_ref[...] = mm(off[...], own)


def root_kernel(z, spb, UPD, ROWS, RR, RL, E, own_rows, off, x_ref, lift_ref, side, xt_ref):
    W0, span = E.shape
    p, n = RR.shape[-2:]
    h = UPD.shape[-2]
    b1 = h * z.C
    for g in range(z.G):
        for r in range(z.R):
            for c in range(z.C):
                at = ((g * z.R + r) * z.C + c) * p
                side[at : at + p] = RR[c % CORES, g, c // CORES, r]
    packed = []
    for g in range(z.G):
        u = jnp.concatenate(
            [UPD[c % CORES, g, c // CORES, r] for r in range(z.R) for c in range(z.C)], axis=0
        )
        packed.append(
            (
                jnp.concatenate(split(u), axis=1),
                jnp.concatenate([ROWS[g, r] for r in range(z.R)], axis=1),
            )
        )

    def block(k, j):
        pieces = []
        for s in range(spb):
            idx = spb * (k * (k - 1) // 2) + s * k + j
            pieces += [RL[q, idx] for q in range(RL.shape[0])]
        return jnp.concatenate(pieces, axis=0)

    ys = []
    for k in range(z.C):
        res = side[k * span : (k + 1) * span]
        for w, rows in packed:
            ids = lax.broadcasted_iota(jnp.int32, (span, rows.shape[1]), 0) + k * span
            hot = jnp.where(ids == rows, 1.0, 0.0).astype(jnp.bfloat16)
            both = bdot(hot, w)
            res = res - (both[:, :n] + both[:, n:])
        for j in range(k):
            res = res - mm(block(k, j), ys[j])
        ys.append(mm(E[k * span : (k + 1) * span], res))
    xs = [None] * z.C
    for k in reversed(range(z.C)):
        res = ys[k].T
        for i in range(k + 1, z.C):
            res = res - tmm(xs[i], block(i, k))
        xs[k] = tmm(res, E[k * span : (k + 1) * span])
        side[k * span : (k + 1) * span] = xs[k].T
    g, r, c = here()
    flat = (g * z.R + r) * z.C + c
    x_ref[...] = side[pl.ds(flat * p, p)]
    picked = jnp.zeros((n, b1), jnp.float32)
    for k in range(z.C):
        ids = lax.broadcasted_iota(jnp.int32, (span, b1), 0) + k * span
        hot = jnp.where(ids == own_rows[...], 1.0, 0.0).astype(jnp.bfloat16)
        both = bdot(jnp.concatenate(split(xs[k]), axis=0), hot)
        picked = picked + both[:n] + both[n:]
    lift_ref[...] = tmm(picked, off[...])


def backward_kernel(z, GL, inv, y_ref, lift, out_ref, xs_ref):
    b1 = inv.shape[1]
    xs = [None] * z.R
    for k in reversed(range(z.R)):
        lk = jnp.concatenate([lift[k % CORES, k // CORES, r] for r in range(z.R)], axis=0)
        res = y_ref[k * b1 : (k + 1) * b1].T - lk
        for i in range(k + 1, z.R):
            res = res - tmm(xs[i], group_block(GL, i, k))
        xs[k] = tmm(res, inv[k * b1 : (k + 1) * b1])
        xs_ref[k * b1 : (k + 1) * b1] = xs[k].T
    r = lax.axis_index("row")
    out_ref[...] = xs_ref[pl.ds(pl.multiple_of(r * b1, 8), b1)]


def on_chip(body, out_shape, scratch, name, *args):
    return pl.pallas_call(
        body,
        out_shape=out_shape,
        scratch_shapes=scratch,
        compiler_params=pltpu.CompilerParams(vmem_limit_bytes=VMEM_BYTES),
        name=name,
    )(*args)


def local(z, group_rhs, group_lower, group_diag_inv, group_offdiag, group_rows, root_rhs, root_lower, root_diag_inv):
    f32 = jnp.float32
    b1, n = group_rhs.shape[1:]
    width = group_diag_inv.shape[1]
    W0, span = root_diag_inv.shape
    strip = root_lower.shape[0]
    spb = span // strip
    inv, off = group_diag_inv[0], group_offdiag[0]
    with_root = strip % (8 * z.G * z.C) == 0
    got = gather_all(
        z, spb, with_root, group_lower[0], group_rhs[0], group_rows, root_rhs, inv, off, root_lower
    )
    GL, ROWS, RR, y, UPD = got[:5]
    if with_root:
        RL = got[5].reshape((z.G * z.C,) + got[5].shape[3:])
    else:
        whole = lax.all_gather(root_lower, ("grp", "row", "col"))
        whole = whole.reshape(z.G * z.R, z.C, strip, span)
        RL = jnp.stack(
            [whole[k * spb + s, j] for k in range(z.C) for s in range(spb) for j in range(k)]
        )[None]
    GL = GL.reshape((z.C,) + GL.shape[2:])
    root_x, lift = on_chip(
        functools.partial(root_kernel, z, spb),
        [jax.ShapeDtypeStruct(root_rhs.shape, f32), jax.ShapeDtypeStruct((n, b1), f32)],
        [pltpu.VMEM((W0, n), f32), pltpu.VMEM((n, W0), f32)],
        "root_solve", UPD, ROWS, RR, RL, root_diag_inv, group_rows, off,
    )
    lifted = exchange_lifted(z, lift)
    out = on_chip(
        functools.partial(backward_kernel, z),
        jax.ShapeDtypeStruct((b1, n), f32),
        [pltpu.VMEM((width, n), f32)],
        "group_backward", GL, inv, y, lifted,
    )
    return out[None], root_x


def solution(mesh):
    z = Sizes(mesh.shape)
    placed = (
        P("grp", "row", None),
        P("grp", "row", "col"),
        P("grp", None, None),
        P("grp", "row", "col"),
        P("grp", "row"),
        P(("grp", "row", "col"), None),
        P(("grp", "row"), "col"),
        P(),
    )
    return jax.shard_map(
        functools.partial(local, z),
        mesh=mesh,
        in_specs=placed,
        out_specs=(P("grp", "row", None), P(("grp", "row", "col"), None)),
        check_vma=False,
    )
```
